512 devices in a mesh: gx: 8 (over y_hi, core), gy: 8 (over y_lo, x), gz: 8 (over z).
Axes of the slice: x: 4, y: 8 (y_hi: 4, y_lo: 2; y = y_hi * 2 + y_lo), z: 8, core: 2. Of those that a mesh axis runs over, the one named last changes fastest.
Arguments:
- populations: float32 [19, 32, 64, 1024], P(None, 'gz', 'gy', 'gx'), as said below
- porosity: float32 [32, 64, 1024], P('gz', 'gy', 'gx'), may hold values from 0 to 1
- node_type: int32 [32, 64, 1024], P('gz', 'gy', 'gx'), may hold values from 0 to 3, as said below
- step_index: int32 [1], replicated, may hold values from 0 to 4095
- adjoint_end: float32 [19, 32, 64, 1024], P(None, 'gz', 'gy', 'gx'), may hold values from -6 to 6
Outputs:
- adjoint_start: float32 [19, 32, 64, 1024], P(None, 'gz', 'gy', 'gx')
- sensitivity: float32 [32, 64, 1024], P('gz', 'gy', 'gx')
The draws below stay inside these ranges and needn't reach their ends.
Inputs may be any that keep to these rules, and one draw needn't show every extreme that they name: `populations`: every entry is positive, between 0.4 and 1.9 times its velocity's weight. `node_type`: cells of the first and last planes across the span and along the depth are walls, as are scattered obstacle cells; the other cells of the first plane along the stream are inlets, of the last plane outlets.
All inputs are finite; a program needn't handle non-finite values.
Results may differ from the reference program's by a relative error of at most 0.0001.
Values sent between devices are 32-bit elements; how exact they have to be, the bound alone decides.
No kernel may reach another device: no remote copies, remote signals or barrier semaphores. Data moves between devices by JAX's collectives and lax.ppermute only.
A program may use at most 64 MiB of HBM per device.

```python
import math
import jax
import jax.numpy as jnp
from jax import lax

Q = 19
STEPS = 2
NX = 1024
NY = 64
NZ = 32


lattice_velocities = ((0, 0, 0), (1, 0, 0), (-1, 0, 0), (0, 1, 0), (0, -1, 0), (0, 0, 1), (0, 0, -1), (1, 1, 0), (-1, -1, 0), (1, -1, 0), (-1, 1, 0), (1, 0, 1), (-1, 0, -1), (1, 0, -1), (-1, 0, 1), (0, 1, 1), (0, -1, -1), (0, 1, -1), (0, -1, 1))


lattice_weights = (1.0 / 3.0,) + (1.0 / 18.0,) * 6 + (1.0 / 36.0,) * 12


def draw_populations(key, part):
    key = jax.random.fold_in(key, 11)
    column_east = jnp.asarray([vector[0] for vector in lattice_velocities], jnp.float32)[:, None, None, None]
    weight_column = jnp.asarray(lattice_weights, jnp.float32)[:, None, None, None]
    projected = 0.1 * column_east
    baseline = weight_column * (1.0 + 3.0 * projected + 4.5 * projected * projected - 0.015)
    factor = jax.random.uniform(key, (Q, NZ, NY, NX), jnp.float32, 2.0 / 3.0, 4.0 / 3.0)
    return (baseline * factor).astype(jnp.float32)


def draw_node_type(key, part):
    key = jax.random.fold_in(key, 23)
    depth_pos = jnp.arange(NZ)[:, None, None]
    span_pos = jnp.arange(NY)[None, :, None]
    stream_pos = jnp.arange(NX)[None, None, :]
    obstacle = jax.random.randint(key, (NZ, NY, NX), 0, 10) == 0
    walled = (span_pos == 0) | (span_pos == NY - 1) | (depth_pos == 0) | (depth_pos == NZ - 1) | obstacle
    inlet_plane = (stream_pos == 0) & (span_pos == 1) | (stream_pos == 0)
    outlet_plane = stream_pos == NX - 1
    kinds = jnp.where(walled, 1, jnp.where(inlet_plane, 2, jnp.where(outlet_plane, 3, 0)))
    kinds = jnp.where((depth_pos == 1) & (span_pos == 1) & outlet_plane, 3, kinds)
    return kinds.astype(jnp.int32)


def block_levels(own_key, shape, shards, least, largest):
    factor_of, own = 1.0, jax.random.fold_in(own_key, 6)
    for position, blocks in shards:
        draws = jnp.exp(jax.random.uniform(jax.random.fold_in(own, position), (blocks,), jnp.float32, least / len(shards), largest / len(shards)))
        factor_of = factor_of * jnp.repeat(draws, shape[position] // blocks).reshape([-1 if axis == position else 1 for axis in range(len(shape))])
    return factor_of


def normal_values(key, extent, deviation, bound, cuts=(), held_as=jnp.bfloat16):
    values = jax.random.normal(key, extent, jnp.float32) * deviation
    if len(cuts) > 0:
        values = block_levels(key, extent, cuts, -0.22, 0.18) * values
    return jnp.clip(values, min=-bound, max=bound).astype(held_as)


def setup_inputs(seed: int = 0) -> dict:
    streams_of = jax.random.split(jax.random.key(seed), 6)
    return {
        "populations": draw_populations(jax.random.fold_in(streams_of[5], 71), 0),
        "porosity": jnp.clip(1.0 * jax.random.uniform(streams_of[1], (NZ, NY, NX), jnp.float32) ** block_levels(streams_of[1], (NZ, NY, NX), ((0, 8), (1, 8), (2, 8)), -0.2, 0.2), 0.0, 1.0),
        "node_type": draw_node_type(jax.random.fold_in(streams_of[5], 71), 0),
        "step_index": jax.random.randint(streams_of[3], (1,), 0, 4096).astype(jnp.int32),
        "adjoint_end": normal_values(streams_of[4], (Q, NZ, NY, NX), 1.0, 6.0, ((1, 8), (2, 8), (3, 8)), jnp.float32),
    }


lattice_velocities = ((0, 0, 0), (1, 0, 0), (-1, 0, 0), (0, 1, 0), (0, -1, 0), (0, 0, 1), (0, 0, -1), (1, 1, 0), (-1, -1, 0), (1, -1, 0), (-1, 1, 0), (1, 0, 1), (-1, 0, -1), (1, 0, -1), (-1, 0, 1), (0, 1, 1), (0, -1, -1), (0, 1, -1), (0, -1, 1))
lattice_weights = (1.0 / 3.0,) + (1.0 / 18.0,) * 6 + (1.0 / 36.0,) * 12
opposite_index = (0, 2, 1, 4, 3, 6, 5, 8, 7, 10, 9, 12, 11, 14, 13, 16, 15, 18, 17)
relax_rate = 1.25
ramp_factor = 0.1
inlet_base = 0.1
inlet_period = 64.0

def lattice_column(which):
    return jnp.asarray([vector[which] for vector in lattice_velocities], jnp.float32)[:, None, None, None]

def weight_column():
    return jnp.asarray(lattice_weights, jnp.float32)[:, None, None, None]

def equilibrium(density, flow_east, flow_north, flow_depth):
    projected = lattice_column(0) * flow_east + lattice_column(1) * flow_north + lattice_column(2) * flow_depth
    square = flow_east * flow_east + flow_north * flow_north + flow_depth * flow_depth
    return weight_column() * density * (1.0 + 3.0 * projected + 4.5 * projected * projected - 1.5 * square)

def collide(current, porosity, node_kinds, inlet_speed):
    density = lax.optimization_barrier(jnp.sum(current, axis=0))
    flow_east = lax.optimization_barrier(jnp.sum(lattice_column(0) * current, axis=0)) / density
    flow_north = lax.optimization_barrier(jnp.sum(lattice_column(1) * current, axis=0)) / density
    flow_depth = lax.optimization_barrier(jnp.sum(lattice_column(2) * current, axis=0)) / density
    damping = ramp_factor * (1.0 - porosity) / (ramp_factor + porosity)
    retained = 1.0 - damping
    relaxed = current - relax_rate * (current - equilibrium(density, retained * flow_east, retained * flow_north, retained * flow_depth))
    bounced = current[jnp.asarray(opposite_index)]
    unit_field = jnp.ones_like(density)
    inflow = equilibrium(unit_field, inlet_speed * unit_field, 0.0 * unit_field, 0.0 * unit_field)
    outflow = equilibrium(density, flow_east, flow_north, flow_depth)
    collided = jnp.where(node_kinds == 1, bounced, jnp.where(node_kinds == 2, inflow, jnp.where(node_kinds == 3, outflow, relaxed)))
    kinetic = flow_east * flow_east + flow_north * flow_north + flow_depth * flow_depth
    energy = jnp.where(node_kinds == 0, damping * density * kinetic, 0.0 * density)
    return (collided, energy)

def inlet_value(step_index, offset):
    moment = (step_index[0] + offset).astype(jnp.float32)
    return inlet_base * (1.0 + 0.8 * jnp.sin(2.0 * math.pi * moment / inlet_period))

def stream_periodic(field, sign):
    slabs = []
    for q in range(len(lattice_velocities)):
        vector = lattice_velocities[q]
        slabs.append(jnp.roll(field[q], (sign * vector[2], sign * vector[1], sign * vector[0]), axis=(0, 1, 2)))
    return jnp.stack(slabs)

def reference(populations, porosity, node_type, step_index, adjoint_end):
    states = []
    current = populations
    for t in range(STEPS):
        states.append(current)
        if t + 1 < STEPS:
            collided, energy = collide(current, porosity, node_type, inlet_value(step_index, t))
            current = stream_periodic(collided, 1)
    adjoint = adjoint_end
    sensitivity = jnp.zeros_like(porosity)
    for t in reversed(range(STEPS)):
        arriving = stream_periodic(adjoint, -1)
        inlet_speed = inlet_value(step_index, t)

        def local_step(incoming, design):
            return collide(incoming, design, node_type, inlet_speed)
        collided, pullback = jax.vjp(local_step, states[t], porosity)
        adjoint, design_grad = pullback((arriving, jnp.ones_like(porosity)))
        sensitivity = sensitivity + design_grad
    return (adjoint, sensitivity)
```

```python
import math

import jax
import jax.numpy as jnp
from jax import lax
from jax.sharding import PartitionSpec as P

VELOCITIES = (
    (0, 0, 0),
    (1, 0, 0),
    (-1, 0, 0),
    (0, 1, 0),
    (0, -1, 0),
    (0, 0, 1),
    (0, 0, -1),
    (1, 1, 0),
    (-1, -1, 0),
    (1, -1, 0),
    (-1, 1, 0),
    (1, 0, 1),
    (-1, 0, -1),
    (1, 0, -1),
    (-1, 0, 1),
    (0, 1, 1),
    (0, -1, -1),
    (0, 1, -1),
    (0, -1, 1),
)
WEIGHTS = (1.0 / 3.0,) + (1.0 / 18.0,) * 6 + (1.0 / 36.0,) * 12
OPPOSITE = (0, 2, 1, 4, 3, 6, 5, 8, 7, 10, 9, 12, 11, 14, 13, 16, 15, 18, 17)
Q = 19
RATE = 1.25
RAMP = 0.1


def add_up(terms):
    total = None
    for sign, value in terms:
        if total is None:
            total = value if sign > 0 else -value
        else:
            total = total + value if sign > 0 else total - value
    return total


def moments(f):
    density = add_up([(1, f[q]) for q in range(Q)])
    flow = [
        add_up([(VELOCITIES[q][i], f[q]) for q in range(Q) if VELOCITIES[q][i]])
        for i in range(3)
    ]
    return density, flow


def along(q, vector):
    return add_up([(VELOCITIES[q][i], vector[i]) for i in range(3) if VELOCITIES[q][i]])


def damping_of(porosity):
    return RAMP * (1.0 - porosity) / (RAMP + porosity)


def collide(f, porosity, kinds, speed):
    density, flow = moments(f)
    inverse = 1.0 / density
    kept = jnp.where(kinds == 0, 1.0 - damping_of(porosity), 1.0)
    inlet = kinds == 2
    v = [jnp.where(inlet, speed if i == 0 else 0.0, flow[i] * inverse * kept) for i in range(3)]
    r = jnp.where(inlet, 1.0, density)
    fluid = kinds == 0
    wall = kinds == 1
    scale = jnp.where(fluid, RATE, 1.0) * r
    keep = jnp.where(fluid, 1.0 - RATE, 0.0)
    base = 1.0 - 1.5 * (v[0] * v[0] + v[1] * v[1] + v[2] * v[2])
    out = []
    for q in range(Q):
        p = along(q, v)
        shape = base if p is None else base + p * (3.0 + 4.5 * p)
        out.append(jnp.where(wall, f[OPPOSITE[q]], keep * f[q] + (WEIGHTS[q] * scale) * shape))
    return out


def pull_back(density, flow, h, porosity, kinds):
    fluid = kinds == 0
    wall = kinds == 1
    outlet = kinds == 3
    inverse = 1.0 / density
    u = [flow[i] * inverse for i in range(3)]
    square = u[0] * u[0] + u[1] * u[1] + u[2] * u[2]
    ramp = 1.0 / (RAMP + porosity)
    damping = jnp.where(fluid, RAMP * (1.0 - porosity) * ramp, 0.0)
    kept = 1.0 - damping
    v = [kept * u[i] for i in range(3)]
    wh = [WEIGHTS[q] * h[q] for q in range(Q)]
    zero, first = moments(wh)
    second = {}
    for i in range(3):
        for j in range(i, 3):
            second[i, j] = second[j, i] = add_up(
                [
                    (VELOCITIES[q][i] * VELOCITIES[q][j], wh[q])
                    for q in range(Q)
                    if VELOCITIES[q][i] * VELOCITIES[q][j]
                ]
            )
    bent = [
        4.5 * (second[i, 0] * v[0] + second[i, 1] * v[1] + second[i, 2] * v[2]) - 1.5 * zero * v[i]
        for i in range(3)
    ]
    slope = [3.0 * first[i] + 2.0 * bent[i] for i in range(3)]
    level = zero + sum(v[i] * (3.0 * first[i] + bent[i]) for i in range(3))
    rate = jnp.where(fluid, RATE, jnp.where(outlet, 1.0, 0.0))
    keep = jnp.where(fluid, 1.0 - RATE, 0.0)
    turn = sum(slope[i] * u[i] for i in range(3))
    tilt = [rate * kept * slope[i] + 2.0 * damping * u[i] for i in range(3)]
    flat = rate * (level - kept * turn) - damping * square
    out = []
    for q in range(Q):
        p = along(q, tilt)
        moved = keep * h[q] + (flat if p is None else flat + p)
        out.append(jnp.where(wall, h[OPPOSITE[q]], moved))
    by_porosity = jnp.where(
        fluid,
        (-RAMP * (1.0 + RAMP)) * ramp * ramp * density * (square - RATE * turn),
        0.0,
    )
    return out, by_porosity


def with_halo(block, axis, dim, width):
    count = lax.axis_size(axis)
    forward = [(i, (i + 1) % count) for i in range(count)]
    backward = [(t, s) for s, t in forward]
    low = lax.ppermute(
        lax.slice_in_dim(block, block.shape[dim] - width, None, axis=dim), axis, forward
    )
    high = lax.ppermute(lax.slice_in_dim(block, 0, width, axis=dim), axis, backward)
    return jnp.concatenate([low, block, high], axis=dim)


def shifted(field, shift):
    return field[
        tuple(slice(1 - s, field.shape[i] - 1 - s) for i, s in enumerate(reversed(shift)))
    ]


def inner(field):
    return field[1:-1, 1:-1, 1:-1]


def on_device(populations, porosity, node_type, step_index, adjoint_end):
    moment = step_index[0].astype(jnp.float32)
    speed = 0.1 * (1.0 + 0.8 * jnp.sin(2.0 * math.pi * moment / 64.0))
    f = [populations[q] for q in range(Q)]
    collided = collide(f, porosity, node_type, speed)
    whole = jnp.concatenate(
        [
            jnp.stack(collided),
            adjoint_end,
            porosity[None],
            node_type.astype(jnp.float32)[None],
        ]
    )
    for axis, dim in (("gz", 1), ("gy", 2), ("gx", 3)):
        whole = with_halo(whole, axis, dim, 2)
    later = [shifted(whole[q], VELOCITIES[q]) for q in range(Q)]
    h = [shifted(whole[Q + q], tuple(-c for c in VELOCITIES[q])) for q in range(Q)]
    design, kinds = inner(whole[2 * Q]), inner(whole[2 * Q + 1])
    density, flow = moments(later)
    adjoint, sense = pull_back(density, flow, h, design, kinds)
    h = [shifted(adjoint[q], tuple(-c for c in VELOCITIES[q])) for q in range(Q)]
    density, flow = moments(f)
    adjoint, by_porosity = pull_back(density, flow, h, porosity, node_type)
    return jnp.stack(adjoint), inner(sense) + by_porosity


def solution(mesh):
    brick = P(None, "gz", "gy", "gx")
    field = P("gz", "gy", "gx")
    return jax.shard_map(
        on_device,
        mesh=mesh,
        in_specs=(brick, field, field, P(), brick),
        out_specs=(brick, field),
        check_vma=False,
    )
```

```python
import math

import jax
import jax.numpy as jnp
from jax import lax
from jax.experimental import pallas as pl
from jax.experimental.pallas import tpu as pltpu
from jax.sharding import PartitionSpec as P

VELOCITIES = (
    (0, 0, 0),
    (1, 0, 0),
    (-1, 0, 0),
    (0, 1, 0),
    (0, -1, 0),
    (0, 0, 1),
    (0, 0, -1),
    (1, 1, 0),
    (-1, -1, 0),
    (1, -1, 0),
    (-1, 1, 0),
    (1, 0, 1),
    (-1, 0, -1),
    (1, 0, -1),
    (-1, 0, 1),
    (0, 1, 1),
    (0, -1, -1),
    (0, 1, -1),
    (0, -1, 1),
)
WEIGHTS = (1.0 / 3.0,) + (1.0 / 18.0,) * 6 + (1.0 / 36.0,) * 12
OPPOSITE = (0, 2, 1, 4, 3, 6, 5, 8, 7, 10, 9, 12, 11, 14, 13, 16, 15, 18, 17)
Q = 19
RATE = 1.25
RAMP = 0.1
NZ, NY, NX = 4, 8, 128
EXT = NZ + 2
LOW, HIGH = EXT, EXT + 1
SIDES = EXT + 2
ROWS = 8

FORWARD, ADJOINT, DESIGN, KIND = range(4)


def opposed(c):
    return tuple(-i for i in c)


Z_FIELDS = (
    [(FORWARD, q, VELOCITIES[q][2]) for q in range(Q)]
    + [(ADJOINT, q, -VELOCITIES[q][2]) for q in range(Q)]
    + [(DESIGN, 0, 0), (KIND, 0, 0)]
)
Z_UP, Z_DOWN = [], []
for _what, _which, _s in Z_FIELDS:
    if _s >= 0:
        Z_UP += [(_what, _which, p) for p in range(NZ - 1 - _s, NZ)]
    if _s <= 0:
        Z_DOWN += [(_what, _which, p) for p in range(0, 1 - _s)]
Z_UP_AT = {entry: i for i, entry in enumerate(Z_UP)}
Z_DOWN_AT = {entry: i for i, entry in enumerate(Z_DOWN)}

Y_FIELDS = []
for _cy in (-1, 0, 1):
    for _cx in (-1, 0, 1):
        _same = [q for q in range(Q) if VELOCITIES[q][:2] == (_cx, _cy)]
        Y_FIELDS.append((FORWARD, (_cx, _cy, 0), [(1, q) for q in _same], _cy))
        _deep = [(VELOCITIES[q][2], q) for q in _same if VELOCITIES[q][2]]
        if _deep:
            Y_FIELDS.append((FORWARD, (_cx, _cy, 1), _deep, _cy))
Y_FIELDS += [(ADJOINT, q, [(1, q)], -VELOCITIES[q][1]) for q in range(Q)]
Y_FIELDS += [(DESIGN, 0, [(1, 0)], 0), (KIND, 0, [(1, 0)], 0)]
Y_AT = {(what, which): i for i, (what, which, _, _) in enumerate(Y_FIELDS)}
Y_UP, Y_DOWN = [], []
for _i, (_, _, _, _s) in enumerate(Y_FIELDS):
    if _s >= 0:
        Y_UP += [(_i, row) for row in range(NY - 1 - _s, NY)]
    if _s <= 0:
        Y_DOWN += [(_i, row) for row in range(0, 1 - _s)]
Y_UP_AT = {entry: i for i, entry in enumerate(Y_UP)}
Y_DOWN_AT = {entry: i for i, entry in enumerate(Y_DOWN)}


def padded(rows):
    return -(-(rows + 2) // ROWS) * ROWS


Y_UP_ROWS, Y_DOWN_ROWS = padded(len(Y_UP) * EXT), padded(len(Y_DOWN) * EXT)

X_FIELDS = []
for _s in (1, -1, 0):
    X_FIELDS += [(FORWARD, (_s, i)) for i in range(3)]
    X_FIELDS += [(ADJOINT, q) for q in range(Q) if -VELOCITIES[q][0] == _s]
X_FIELDS += [(DESIGN, 0), (KIND, 0)]
X_AT = {entry: i for i, entry in enumerate(X_FIELDS)}
PER_TILE = 4
PACKED = -(-len(X_FIELDS) // PER_TILE)


def shift_of(entry):
    what, which = entry
    if what == FORWARD:
        return which[0]
    return -VELOCITIES[which][0] if what == ADJOINT else 0


def add_up(terms):
    total = None
    for sign, value in terms:
        if total is None:
            total = value if sign > 0 else -value
        else:
            total = total + value if sign > 0 else total - value
    return total


def moments(f):
    density = add_up([(1, f[q]) for q in range(Q)])
    flow = [
        add_up([(VELOCITIES[q][i], f[q]) for q in range(Q) if VELOCITIES[q][i]])
        for i in range(3)
    ]
    return density, flow


def along(q, vector):
    return add_up([(VELOCITIES[q][i], vector[i]) for i in range(3) if VELOCITIES[q][i]])


def collide(f, porosity, kinds, speed):
    density, flow = moments(f)
    inverse = 1.0 / density
    fluid = kinds == 0
    wall = kinds == 1
    inlet = kinds == 2
    damping = RAMP * (1.0 - porosity) / (RAMP + porosity)
    kept = jnp.where(fluid, 1.0 - damping, 1.0)
    v = [
        jnp.where(inlet, speed if i == 0 else 0.0, flow[i] * inverse * kept)
        for i in range(3)
    ]
    r = jnp.where(inlet, 1.0, density)
    scale = jnp.where(fluid, RATE, 1.0) * r
    keep = jnp.where(fluid, 1.0 - RATE, 0.0)
    base = 1.0 - 1.5 * (v[0] * v[0] + v[1] * v[1] + v[2] * v[2])
    out = []
    for q in range(Q):
        p = along(q, v)
        shape = base if p is None else base + p * (3.0 + 4.5 * p)
        moved = keep * f[q] + (WEIGHTS[q] * scale) * shape
        out.append(jnp.where(wall, f[OPPOSITE[q]], moved))
    return out


def pull_back(density, flow, h, porosity, kinds, wanted):
    fluid = kinds == 0
    wall = kinds == 1
    outlet = kinds == 3
    inverse = 1.0 / density
    u = [flow[i] * inverse for i in range(3)]
    square = u[0] * u[0] + u[1] * u[1] + u[2] * u[2]
    ramp = 1.0 / (RAMP + porosity)
    damping = jnp.where(fluid, RAMP * (1.0 - porosity) * ramp, 0.0)
    kept = 1.0 - damping
    v = [kept * u[i] for i in range(3)]
    face, edge = WEIGHTS[1], WEIGHTS[7]
    plus = {}
    minus = {}
    for q in range(1, Q, 2):
        plus[q] = h[q] + h[q + 1]
        minus[q] = h[q] - h[q + 1]
    xy, yx, xz, zx, yz, zy = (plus[q] for q in (7, 9, 11, 13, 15, 17))
    second = [
        [face * plus[1] + edge * ((xy + yx) + (xz + zx)), edge * (xy - yx), edge * (xz - zx)],
        [None, face * plus[3] + edge * ((xy + yx) + (yz + zy)), edge * (yz - zy)],
        [None, None, face * plus[5] + edge * ((xz + zx) + (yz + zy))],
    ]
    second[1][0], second[2][0], second[2][1] = second[0][1], second[0][2], second[1][2]
    zero = (
        WEIGHTS[0] * h[0]
        + face * (plus[1] + plus[3] + plus[5])
        + edge * ((xy + yx) + (xz + zx) + (yz + zy))
    )
    first = [
        face * minus[1] + edge * ((minus[7] + minus[9]) + (minus[11] + minus[13])),
        face * minus[3] + edge * ((minus[7] - minus[9]) + (minus[15] + minus[17])),
        face * minus[5] + edge * ((minus[11] - minus[13]) + (minus[15] - minus[17])),
    ]
    bent = [
        4.5 * (second[i][0] * v[0] + second[i][1] * v[1] + second[i][2] * v[2])
        - 1.5 * zero * v[i]
        for i in range(3)
    ]
    level = zero + sum(v[i] * (3.0 * first[i] + bent[i]) for i in range(3))
    slope = [3.0 * first[i] + 2.0 * bent[i] for i in range(3)]
    rate = jnp.where(fluid, RATE, jnp.where(outlet, 1.0, 0.0))
    keep = jnp.where(fluid, 1.0 - RATE, 0.0)
    turn = sum(slope[i] * u[i] for i in range(3))
    moved_rate = rate * kept
    tilt = [moved_rate * slope[i] + 2.0 * damping * u[i] for i in range(3)]
    flat = rate * level - moved_rate * turn - damping * square
    out = {}
    for q in wanted:
        p = along(q, tilt)
        moved = keep * h[q] + (flat if p is None else flat + p)
        out[q] = jnp.where(wall, h[OPPOSITE[q]], moved)
    by_porosity = jnp.where(
        fluid,
        (-RAMP * (1.0 + RAMP)) * ramp * ramp * density * (square - RATE * turn),
        0.0,
    )
    return out, by_porosity


def collide_kernel(step, pop, adj, por, kind, moved, up, down):
    moment = jnp.full((NY, NX), step[0] & 63, jnp.int32).astype(jnp.float32)
    speed = 0.1 * (1.0 + 0.8 * jnp.sin((2.0 * math.pi / 64.0) * moment))
    for z in range(NZ):
        kinds = kind[z]
        design = por[z]
        collided = collide([pop[q, z] for q in range(Q)], design, kinds, speed)
        for q in range(Q):
            moved[q, z] = collided[q]

        def value(what, which):
            if what == FORWARD:
                return collided[which]
            if what == ADJOINT:
                return adj[which, z]
            return design if what == DESIGN else kinds.astype(jnp.float32)

        for table, out in ((Z_UP_AT, up), (Z_DOWN_AT, down)):
            for (what, which, plane), at in table.items():
                if plane == z:
                    out[at] = value(what, which)


def rows_kernel(moved, adj, por, kind, below, above, shifted, up, down):
    def plane_of(what, which, z):
        if z < 0:
            return below[Z_UP_AT[what, which, z + NZ]]
        if z >= NZ:
            return above[Z_DOWN_AT[what, which, z - NZ]]
        if what == FORWARD:
            return moved[which, z]
        if what == ADJOINT:
            return adj[which, z]
        return por[z] if what == DESIGN else kind[z].astype(jnp.float32)

    for i, (what, _, parts, _) in enumerate(Y_FIELDS):
        for t in range(EXT):
            terms = []
            for sign, q in parts:
                s = VELOCITIES[q][2] if what == FORWARD else 0
                if what == ADJOINT:
                    s = -VELOCITIES[q][2]
                terms.append((sign, plane_of(what, q, t - 1 - s)))
            shifted[pl.ds((i * EXT + t) * ROWS, ROWS), :] = add_up(terms)
    for table, out in ((Y_UP, up), (Y_DOWN, down)):
        for at, (i, row) in enumerate(table):
            out[pl.ds(at * EXT, EXT), :] = shifted[
                pl.ds(i * EXT * ROWS + row, EXT, stride=ROWS), :
            ]
        used = len(table) * EXT
        out[pl.ds(used, out.shape[0] - used), :] = jnp.zeros(
            (out.shape[0] - used, NX), jnp.float32
        )


def columns_kernel(shifted, up, down, left, right, wide, packed):
    row = lax.broadcasted_iota(jnp.int32, (NY, NX), 0)
    lane = lax.broadcasted_iota(jnp.int32, (NY, NX), 1)

    def rows_of(ref, at):
        return ref[pl.ds(at * EXT, ROWS), :]

    def row_of(ref, at, t):
        return jnp.broadcast_to(ref[pl.ds(at * EXT + t, 1), :], (NY, NX))

    def tile_of(entry, t):
        i = Y_AT[entry]
        s = Y_FIELDS[i][3]
        if t == LOW:
            if s < 0:
                return rows_of(down, Y_DOWN_AT[i, 0])
            return rows_of(left, Y_UP_AT[i, NY - 1 - s])
        if t == HIGH:
            if s > 0:
                return rows_of(up, Y_UP_AT[i, NY - 1])
            return rows_of(right, Y_DOWN_AT[i, -s])
        own = shifted[pl.ds((i * EXT + t) * ROWS, ROWS), :]
        if s > 0:
            return jnp.where(
                row == 0, row_of(left, Y_UP_AT[i, NY - 1], t), pltpu.roll(own, 1, 0)
            )
        if s < 0:
            return jnp.where(
                row == NY - 1, row_of(right, Y_DOWN_AT[i, 0], t), pltpu.roll(own, NY - 1, 0)
            )
        return own

    for u in range(PACKED):
        total = None
        for j, entry in enumerate(X_FIELDS[u * PER_TILE : (u + 1) * PER_TILE]):
            f = u * PER_TILE + j
            what, which = entry
            for t in range(EXT + 2):
                if what != FORWARD:
                    tile = tile_of(entry, t)
                else:
                    cx, part = which
                    terms = []
                    for cy in (-1, 0, 1):
                        source = (FORWARD, (cx, cy, 1 if part == 2 else 0))
                        if source in Y_AT and (part != 1 or cy):
                            sign = cy if part == 1 else 1
                            terms.append((sign, tile_of(source, t)))
                    tile = add_up(terms)
                wide[pl.ds((f * (EXT + 2) + t) * ROWS, ROWS), :] = tile
                k = j * (EXT + 2) + t
                turned = pltpu.roll(tile, (2 + 4 * k) % NX, 1)
                total = turned if total is None else jnp.where(lane >= 4 * k, turned, total)
        packed[u] = total


def adjoint_kernel(wide, packed, before, after, pop, por, kind, out, sense, states):
    lane = lax.broadcasted_iota(jnp.int32, (NY, NX), 1)
    row = lax.broadcasted_iota(jnp.int32, (NY, NX), 0)
    slot = lane & 3
    beside = [jnp.where(slot < 2, before[u], after[u]) for u in range(PACKED)]

    def value(entry, t):
        f = X_AT[entry]
        u, j = f // PER_TILE, f % PER_TILE
        s = shift_of(entry)
        if t == SIDES:
            if s > 0:
                base = jnp.where(slot == 1, pltpu.roll(beside[u], 1, 1), pltpu.roll(packed[u], 1, 1))
            elif s < 0:
                base = jnp.where(
                    slot == 2, pltpu.roll(beside[u], NX - 1, 1), pltpu.roll(packed[u], NX - 1, 1)
                )
            else:
                base = beside[u]
            return pltpu.roll(base, NX - 32 * j, 1) if j else base
        own = wide[pl.ds((f * (EXT + 2) + t) * ROWS, ROWS), :]
        k = j * (EXT + 2) + t
        if s > 0:
            return jnp.where(
                lane == 0, pltpu.roll(beside[u], NX - (4 * k + 1), 1), pltpu.roll(own, 1, 1)
            )
        if s < 0:
            return jnp.where(
                lane == NX - 1,
                pltpu.roll(beside[u], (NX - 1 - (4 * k + 2)) % NX, 1),
                pltpu.roll(own, NX - 1, 1),
            )
        return own

    def at(q, t):
        return pl.ds((q * (SIDES + 1) + t) * ROWS, ROWS)

    for t in (SIDES, LOW, HIGH, 0, EXT - 1, *range(1, NZ + 1)):
        if t == SIDES:
            wanted = [q for q in range(Q) if VELOCITIES[q][0]]
        elif t in (LOW, HIGH):
            wanted = [q for q in range(Q) if VELOCITIES[q][1] == (1 if t == HIGH else -1)]
        elif t in (0, EXT - 1):
            wanted = [q for q in range(Q) if VELOCITIES[q][2] == (1 if t else -1)]
        else:
            wanted = range(Q)
        parts = {s: [value((FORWARD, (s, i)), t) for i in range(3)] for s in (-1, 0, 1)}
        density = parts[0][0] + parts[1][0] + parts[-1][0]
        flow = [
            parts[1][0] - parts[-1][0],
            parts[0][1] + parts[1][1] + parts[-1][1],
            parts[0][2] + parts[1][2] + parts[-1][2],
        ]
        h = [value((ADJOINT, q), t) for q in range(Q)]
        back, by_porosity = pull_back(
            density, flow, h, value((DESIGN, 0), t), value((KIND, 0), t), wanted
        )
        for q in wanted:
            states[at(q, t), :] = back[q]
        if 1 <= t <= NZ:
            sense[t - 1] = by_porosity

    def moved_x(q, t):
        tile = states[at(q, t), :]
        cx = VELOCITIES[q][0]
        if cx > 0:
            return jnp.where(
                lane == NX - 1,
                pltpu.roll(states[at(q, SIDES), :], (NX - 1 - (4 * t + 2)) % NX, 1),
                pltpu.roll(tile, NX - 1, 1),
            )
        if cx < 0:
            return jnp.where(
                lane == 0,
                pltpu.roll(states[at(q, SIDES), :], NX - (4 * t + 1), 1),
                pltpu.roll(tile, 1, 1),
            )
        return tile

    for z in range(NZ):
        h = []
        for q in range(Q):
            _, cy, cz = VELOCITIES[q]
            t = z + cz + 1
            tile = moved_x(q, t)
            if cy > 0:
                edge = moved_x(q, HIGH)[t : t + 1]
                tile = jnp.where(
                    row == NY - 1, jnp.broadcast_to(edge, (NY, NX)), pltpu.roll(tile, NY - 1, 0)
                )
            elif cy < 0:
                edge = moved_x(q, LOW)[t : t + 1]
                tile = jnp.where(row == 0, jnp.broadcast_to(edge, (NY, NX)), pltpu.roll(tile, 1, 0))
            h.append(tile)
        density, flow = moments([pop[q, z] for q in range(Q)])
        back, by_porosity = pull_back(
            density, flow, h, por[z], kind[z].astype(jnp.float32), range(Q)
        )
        for q in range(Q):
            out[q, z] = back[q]
        sense[z] = sense[z] + by_porosity


VMEM = pl.BlockSpec(memory_space=pltpu.VMEM)
SMEM = pl.BlockSpec(memory_space=pltpu.SMEM)


def call(kernel, shapes, specs, scratch=()):
    out = [jax.ShapeDtypeStruct(shape, jnp.float32) for shape in shapes]
    return pl.pallas_call(
        kernel,
        out_shape=out,
        in_specs=specs,
        out_specs=[VMEM] * len(out),
        scratch_shapes=list(scratch),
        compiler_params=pltpu.CompilerParams(vmem_limit_bytes=12 * 1024 * 1024),
    )


def both_ways(forward, backward, axis):
    count = lax.axis_size(axis)
    ahead = [(i, (i + 1) % count) for i in range(count)]
    behind = [(t, s) for s, t in ahead]
    return lax.ppermute(forward, axis, ahead), lax.ppermute(backward, axis, behind)


def on_device(populations, porosity, node_type, step_index, adjoint_end):
    tile = (NY, NX)
    moved, up, down = call(
        collide_kernel,
        [(Q, NZ, *tile), (len(Z_UP), *tile), (len(Z_DOWN), *tile)],
        [SMEM] + [VMEM] * 4,
    )(step_index, populations, adjoint_end, porosity, node_type)
    below, above = both_ways(up, down, "gz")
    shifted, up, down = call(
        rows_kernel,
        [(len(Y_FIELDS) * EXT * ROWS, NX), (Y_UP_ROWS, NX), (Y_DOWN_ROWS, NX)],
        [VMEM] * 6,
    )(moved, adjoint_end, porosity, node_type, below, above)
    left, right = both_ways(up, down, "gy")
    wide, packed = call(
        columns_kernel,
        [(len(X_FIELDS) * (EXT + 2) * ROWS, NX), (PACKED, *tile)],
        [VMEM] * 5,
    )(shifted, up, down, left, right)
    before, after = both_ways(packed, packed, "gx")
    adjoint, sense = call(
        adjoint_kernel,
        [(Q, NZ, *tile), (NZ, *tile)],
        [VMEM] * 7,
        [pltpu.VMEM((Q * (SIDES + 1) * ROWS, NX), jnp.float32)],
    )(wide, packed, before, after, populations, porosity, node_type)
    return adjoint, sense


def solution(mesh):
    brick = P(None, "gz", "gy", "gx")
    field = P("gz", "gy", "gx")
    return jax.shard_map(
        on_device,
        mesh=mesh,
        in_specs=(brick, field, field, P(), brick),
        out_specs=(brick, field),
        check_vma=False,
    )
```

```python
import functools
import math

import jax
import jax.numpy as jnp
from jax import lax
from jax.experimental import pallas as pl
from jax.experimental.pallas import tpu as pltpu
from jax.sharding import PartitionSpec as P

VELOCITIES = (
    (0, 0, 0),
    (1, 0, 0),
    (-1, 0, 0),
    (0, 1, 0),
    (0, -1, 0),
    (0, 0, 1),
    (0, 0, -1),
    (1, 1, 0),
    (-1, -1, 0),
    (1, -1, 0),
    (-1, 1, 0),
    (1, 0, 1),
    (-1, 0, -1),
    (1, 0, -1),
    (-1, 0, 1),
    (0, 1, 1),
    (0, -1, -1),
    (0, 1, -1),
    (0, -1, 1),
)
WEIGHTS = (1.0 / 3.0,) + (1.0 / 18.0,) * 6 + (1.0 / 36.0,) * 12
OPPOSITE = (0, 2, 1, 4, 3, 6, 5, 8, 7, 10, 9, 12, 11, 14, 13, 16, 15, 18, 17)
Q = 19
RATE = 1.25
RAMP = 0.1
NZ, NY, NX = 4, 8, 128
EXT = NZ + 2
LOW, HIGH = EXT, EXT + 1
SIDES = EXT + 2
ROWS = 8
SWAPPED = ("gx",)

FORWARD, ADJOINT, DESIGN, KIND = range(4)


def opposed(c):
    return tuple(-i for i in c)


Z_FIELDS = (
    [(FORWARD, q, VELOCITIES[q][2]) for q in range(Q)]
    + [(ADJOINT, q, -VELOCITIES[q][2]) for q in range(Q)]
    + [(DESIGN, 0, 0), (KIND, 0, 0)]
)
Z_UP, Z_DOWN = [], []
for _what, _which, _s in Z_FIELDS:
    if _s >= 0:
        Z_UP += [(_what, _which, p) for p in range(NZ - 1 - _s, NZ)]
    if _s <= 0:
        Z_DOWN += [(_what, _which, p) for p in range(0, 1 - _s)]
Z_UP_AT = {entry: i for i, entry in enumerate(Z_UP)}
Z_DOWN_AT = {entry: i for i, entry in enumerate(Z_DOWN)}

Y_FIELDS = []
for _cy in (-1, 0, 1):
    for _cx in (-1, 0, 1):
        _same = [q for q in range(Q) if VELOCITIES[q][:2] == (_cx, _cy)]
        Y_FIELDS.append((FORWARD, (_cx, _cy, 0), [(1, q) for q in _same], _cy))
        _deep = [(VELOCITIES[q][2], q) for q in _same if VELOCITIES[q][2]]
        if _deep:
            Y_FIELDS.append((FORWARD, (_cx, _cy, 1), _deep, _cy))
Y_FIELDS += [(ADJOINT, q, [(1, q)], -VELOCITIES[q][1]) for q in range(Q)]
Y_FIELDS += [(DESIGN, 0, [(1, 0)], 0), (KIND, 0, [(1, 0)], 0)]
Y_AT = {(what, which): i for i, (what, which, _, _) in enumerate(Y_FIELDS)}
Y_UP, Y_DOWN = [], []
for _i, (_, _, _, _s) in enumerate(Y_FIELDS):
    if _s >= 0:
        Y_UP += [(_i, row) for row in range(NY - 1 - _s, NY)]
    if _s <= 0:
        Y_DOWN += [(_i, row) for row in range(0, 1 - _s)]
Y_UP_AT = {entry: i for i, entry in enumerate(Y_UP)}
Y_DOWN_AT = {entry: i for i, entry in enumerate(Y_DOWN)}


def padded(rows):
    return -(-(rows + 2) // ROWS) * ROWS


Y_UP_ROWS, Y_DOWN_ROWS = padded(len(Y_UP) * EXT), padded(len(Y_DOWN) * EXT)

X_FIELDS = []
for _s in (1, -1, 0):
    X_FIELDS += [(FORWARD, (_s, i)) for i in range(3)]
    X_FIELDS += [(ADJOINT, q) for q in range(Q) if -VELOCITIES[q][0] == _s]
X_FIELDS += [(DESIGN, 0), (KIND, 0)]
X_AT = {entry: i for i, entry in enumerate(X_FIELDS)}
PER_TILE = 4
PACKED = -(-len(X_FIELDS) // PER_TILE)


def shift_of(entry):
    what, which = entry
    if what == FORWARD:
        return which[0]
    return -VELOCITIES[which][0] if what == ADJOINT else 0


def add_up(terms):
    total = None
    for sign, value in terms:
        if total is None:
            total = value if sign > 0 else -value
        else:
            total = total + value if sign > 0 else total - value
    return total


def moments(f):
    density = add_up([(1, f[q]) for q in range(Q)])
    flow = [
        add_up([(VELOCITIES[q][i], f[q]) for q in range(Q) if VELOCITIES[q][i]])
        for i in range(3)
    ]
    return density, flow


def along(q, vector):
    return add_up([(VELOCITIES[q][i], vector[i]) for i in range(3) if VELOCITIES[q][i]])


def collide(f, porosity, kinds, speed):
    density, flow = moments(f)
    inverse = 1.0 / density
    fluid = kinds == 0
    wall = kinds == 1
    inlet = kinds == 2
    damping = RAMP * (1.0 - porosity) / (RAMP + porosity)
    kept = jnp.where(fluid, 1.0 - damping, 1.0)
    v = [
        jnp.where(inlet, speed if i == 0 else 0.0, flow[i] * inverse * kept)
        for i in range(3)
    ]
    r = jnp.where(inlet, 1.0, density)
    scale = jnp.where(fluid, RATE, 1.0) * r
    keep = jnp.where(fluid, 1.0 - RATE, 0.0)
    base = 1.0 - 1.5 * (v[0] * v[0] + v[1] * v[1] + v[2] * v[2])
    out = []
    for q in range(Q):
        p = along(q, v)
        shape = base if p is None else base + p * (3.0 + 4.5 * p)
        moved = keep * f[q] + (WEIGHTS[q] * scale) * shape
        out.append(jnp.where(wall, f[OPPOSITE[q]], moved))
    return out


def pull_back(density, flow, h, porosity, kinds, wanted):
    fluid = kinds == 0
    wall = kinds == 1
    outlet = kinds == 3
    inverse = 1.0 / density
    u = [flow[i] * inverse for i in range(3)]
    square = u[0] * u[0] + u[1] * u[1] + u[2] * u[2]
    ramp = 1.0 / (RAMP + porosity)
    damping = jnp.where(fluid, RAMP * (1.0 - porosity) * ramp, 0.0)
    kept = 1.0 - damping
    v = [kept * u[i] for i in range(3)]
    face, edge = WEIGHTS[1], WEIGHTS[7]
    plus = {}
    minus = {}
    for q in range(1, Q, 2):
        plus[q] = h[q] + h[q + 1]
        minus[q] = h[q] - h[q + 1]
    xy, yx, xz, zx, yz, zy = (plus[q] for q in (7, 9, 11, 13, 15, 17))
    second = [
        [face * plus[1] + edge * ((xy + yx) + (xz + zx)), edge * (xy - yx), edge * (xz - zx)],
        [None, face * plus[3] + edge * ((xy + yx) + (yz + zy)), edge * (yz - zy)],
        [None, None, face * plus[5] + edge * ((xz + zx) + (yz + zy))],
    ]
    second[1][0], second[2][0], second[2][1] = second[0][1], second[0][2], second[1][2]
    zero = (
        WEIGHTS[0] * h[0]
        + face * (plus[1] + plus[3] + plus[5])
        + edge * ((xy + yx) + (xz + zx) + (yz + zy))
    )
    first = [
        face * minus[1] + edge * ((minus[7] + minus[9]) + (minus[11] + minus[13])),
        face * minus[3] + edge * ((minus[7] - minus[9]) + (minus[15] + minus[17])),
        face * minus[5] + edge * ((minus[11] - minus[13]) + (minus[15] - minus[17])),
    ]
    bent = [
        4.5 * (second[i][0] * v[0] + second[i][1] * v[1] + second[i][2] * v[2])
        - 1.5 * zero * v[i]
        for i in range(3)
    ]
    level = zero + sum(v[i] * (3.0 * first[i] + bent[i]) for i in range(3))
    slope = [3.0 * first[i] + 2.0 * bent[i] for i in range(3)]
    rate = jnp.where(fluid, RATE, jnp.where(outlet, 1.0, 0.0))
    keep = jnp.where(fluid, 1.0 - RATE, 0.0)
    turn = sum(slope[i] * u[i] for i in range(3))
    moved_rate = rate * kept
    tilt = [moved_rate * slope[i] + 2.0 * damping * u[i] for i in range(3)]
    flat = rate * level - moved_rate * turn - damping * square
    out = {}
    for q in wanted:
        p = along(q, tilt)
        moved = keep * h[q] + (flat if p is None else flat + p)
        out[q] = jnp.where(wall, h[OPPOSITE[q]], moved)
    by_porosity = jnp.where(
        fluid,
        (-RAMP * (1.0 + RAMP)) * ramp * ramp * density * (square - RATE * turn),
        0.0,
    )
    return out, by_porosity


def by_side(axis, act, first, second):
    if axis not in SWAPPED:
        act(first, second)
        return
    here = lax.rem(lax.axis_index(axis), 2)

    @pl.when(here == 0)
    def _():
        act(first, second)

    @pl.when(here == 1)
    def _():
        act(second, first)


def from_side(axis, first, second):
    if axis not in SWAPPED:
        return (lambda at: first[at]), (lambda at: second[at])
    even = lax.rem(lax.axis_index(axis), 2) == 0
    return (
        lambda at: jnp.where(even, second[at], first[at]),
        lambda at: jnp.where(even, first[at], second[at]),
    )


def collide_kernel(
    step, pop_hbm, adj_hbm, por_hbm, kind_hbm, moved, first, second, pop, adj, por, kind, done
):
    copies = [
        pltpu.make_async_copy(source, target, done.at[i])
        for i, (source, target) in enumerate(
            ((pop_hbm, pop), (por_hbm, por), (kind_hbm, kind), (adj_hbm, adj))
        )
    ]
    for copy in copies:
        copy.start()
    moment = jnp.full((NY, NX), step[0] & 63, jnp.int32).astype(jnp.float32)
    speed = 0.1 * (1.0 + 0.8 * jnp.sin((2.0 * math.pi / 64.0) * moment))
    for copy in copies[:3]:
        copy.wait()
    for z in range(NZ):
        collided = collide([pop[q, z] for q in range(Q)], por[z], kind[z], speed)
        for q in range(Q):
            moved[q, z] = collided[q]
    copies[3].wait()

    def value(what, which, z):
        if what == FORWARD:
            return moved[which, z]
        if what == ADJOINT:
            return adj[which, z]
        return por[z] if what == DESIGN else kind[z].astype(jnp.float32)

    def write(up, down):
        for table, out in ((Z_UP_AT, up), (Z_DOWN_AT, down)):
            for entry, at in table.items():
                out[at] = value(*entry)

    by_side("gz", write, first, second)


def copy_both(up, down, first, second):
    for i in range(up.shape[0] // ROWS):
        rows = pl.ds(i * ROWS, ROWS)
        first[rows, :] = up[rows, :]
        second[rows, :] = down[rows, :]


def rows_kernel(moved, adj, por, kind, one, two, shifted, up, down, first, second):
    below, above = from_side("gz", one, two)

    def plane_of(what, which, z):
        if z < 0:
            return below(Z_UP_AT[what, which, z + NZ])
        if z >= NZ:
            return above(Z_DOWN_AT[what, which, z - NZ])
        if what == FORWARD:
            return moved[which, z]
        if what == ADJOINT:
            return adj[which, z]
        return por[z] if what == DESIGN else kind[z].astype(jnp.float32)

    for i, (what, _, parts, _) in enumerate(Y_FIELDS):
        for t in range(EXT):
            terms = []
            for sign, q in parts:
                s = VELOCITIES[q][2] if what == FORWARD else 0
                if what == ADJOINT:
                    s = -VELOCITIES[q][2]
                terms.append((sign, plane_of(what, q, t - 1 - s)))
            shifted[pl.ds((i * EXT + t) * ROWS, ROWS), :] = add_up(terms)
    def write(forward, backward):
        for table, out in ((Y_UP, forward), (Y_DOWN, backward)):
            for at, (i, row) in enumerate(table):
                out[pl.ds(at * EXT, EXT), :] = shifted[
                    pl.ds(i * EXT * ROWS + row, EXT, stride=ROWS), :
                ]
            used = len(table) * EXT
            out[pl.ds(used, out.shape[0] - used), :] = jnp.zeros(
                (out.shape[0] - used, NX), jnp.float32
            )

    write(up, down)
    if "gy" in SWAPPED:
        by_side("gy", functools.partial(copy_both, up, down), first, second)


def columns_kernel(shifted, up, down, one, two, wide, packed):
    left, right = from_side("gy", one, two)
    row = lax.broadcasted_iota(jnp.int32, (NY, NX), 0)
    lane = lax.broadcasted_iota(jnp.int32, (NY, NX), 1)

    def rows_of(ref, at):
        rows = (pl.ds(at * EXT, ROWS), slice(None))
        return ref(rows) if callable(ref) else ref[rows]

    def row_of(ref, at, t):
        return jnp.broadcast_to(ref((pl.ds(at * EXT + t, 1), slice(None))), (NY, NX))

    def tile_of(entry, t):
        i = Y_AT[entry]
        s = Y_FIELDS[i][3]
        if t == LOW:
            if s < 0:
                return rows_of(down, Y_DOWN_AT[i, 0])
            return rows_of(left, Y_UP_AT[i, NY - 1 - s])
        if t == HIGH:
            if s > 0:
                return rows_of(up, Y_UP_AT[i, NY - 1])
            return rows_of(right, Y_DOWN_AT[i, -s])
        own = shifted[pl.ds((i * EXT + t) * ROWS, ROWS), :]
        if s > 0:
            return jnp.where(
                row == 0, row_of(left, Y_UP_AT[i, NY - 1], t), pltpu.roll(own, 1, 0)
            )
        if s < 0:
            return jnp.where(
                row == NY - 1, row_of(right, Y_DOWN_AT[i, 0], t), pltpu.roll(own, NY - 1, 0)
            )
        return own

    for u in range(PACKED):
        total = None
        for j, entry in enumerate(X_FIELDS[u * PER_TILE : (u + 1) * PER_TILE]):
            f = u * PER_TILE + j
            what, which = entry
            for t in range(EXT + 2):
                if what != FORWARD:
                    tile = tile_of(entry, t)
                else:
                    cx, part = which
                    terms = []
                    for cy in (-1, 0, 1):
                        source = (FORWARD, (cx, cy, 1 if part == 2 else 0))
                        if source in Y_AT and (part != 1 or cy):
                            sign = cy if part == 1 else 1
                            terms.append((sign, tile_of(source, t)))
                    tile = add_up(terms)
                wide[pl.ds((f * (EXT + 2) + t) * ROWS, ROWS), :] = tile
                k = j * (EXT + 2) + t
                turned = pltpu.roll(tile, (2 + 4 * k) % NX, 1)
                total = turned if total is None else jnp.where(lane >= 4 * k, turned, total)
        packed[u] = total


def adjoint_kernel(wide, packed, one, two, pop, por, kind, out, sense, states):
    lane = lax.broadcasted_iota(jnp.int32, (NY, NX), 1)
    row = lax.broadcasted_iota(jnp.int32, (NY, NX), 0)
    slot = lane & 3
    before, after = from_side("gx", one, two)
    beside = [jnp.where(slot < 2, before(u), after(u)) for u in range(PACKED)]

    def value(entry, t):
        f = X_AT[entry]
        u, j = f // PER_TILE, f % PER_TILE
        s = shift_of(entry)
        if t == SIDES:
            if s > 0:
                base = jnp.where(slot == 1, pltpu.roll(beside[u], 1, 1), pltpu.roll(packed[u], 1, 1))
            elif s < 0:
                base = jnp.where(
                    slot == 2, pltpu.roll(beside[u], NX - 1, 1), pltpu.roll(packed[u], NX - 1, 1)
                )
            else:
                base = beside[u]
            return pltpu.roll(base, NX - 32 * j, 1) if j else base
        own = wide[pl.ds((f * (EXT + 2) + t) * ROWS, ROWS), :]
        k = j * (EXT + 2) + t
        if s > 0:
            return jnp.where(
                lane == 0, pltpu.roll(beside[u], NX - (4 * k + 1), 1), pltpu.roll(own, 1, 1)
            )
        if s < 0:
            return jnp.where(
                lane == NX - 1,
                pltpu.roll(beside[u], (NX - 1 - (4 * k + 2)) % NX, 1),
                pltpu.roll(own, NX - 1, 1),
            )
        return own

    def at(q, t):
        return pl.ds((q * (SIDES + 1) + t) * ROWS, ROWS)

    for t in (SIDES, LOW, HIGH, 0, EXT - 1, *range(1, NZ + 1)):
        if t == SIDES:
            wanted = [q for q in range(Q) if VELOCITIES[q][0]]
        elif t in (LOW, HIGH):
            wanted = [q for q in range(Q) if VELOCITIES[q][1] == (1 if t == HIGH else -1)]
        elif t in (0, EXT - 1):
            wanted = [q for q in range(Q) if VELOCITIES[q][2] == (1 if t else -1)]
        else:
            wanted = range(Q)
        parts = {s: [value((FORWARD, (s, i)), t) for i in range(3)] for s in (-1, 0, 1)}
        density = parts[0][0] + parts[1][0] + parts[-1][0]
        flow = [
            parts[1][0] - parts[-1][0],
            parts[0][1] + parts[1][1] + parts[-1][1],
            parts[0][2] + parts[1][2] + parts[-1][2],
        ]
        h = [value((ADJOINT, q), t) for q in range(Q)]
        back, by_porosity = pull_back(
            density, flow, h, value((DESIGN, 0), t), value((KIND, 0), t), wanted
        )
        for q in wanted:
            states[at(q, t), :] = back[q]
        if 1 <= t <= NZ:
            sense[t - 1] = by_porosity

    def moved_x(q, t):
        tile = states[at(q, t), :]
        cx = VELOCITIES[q][0]
        if cx > 0:
            return jnp.where(
                lane == NX - 1,
                pltpu.roll(states[at(q, SIDES), :], (NX - 1 - (4 * t + 2)) % NX, 1),
                pltpu.roll(tile, NX - 1, 1),
            )
        if cx < 0:
            return jnp.where(
                lane == 0,
                pltpu.roll(states[at(q, SIDES), :], NX - (4 * t + 1), 1),
                pltpu.roll(tile, 1, 1),
            )
        return tile

    for z in range(NZ):
        h = []
        for q in range(Q):
            _, cy, cz = VELOCITIES[q]
            t = z + cz + 1
            tile = moved_x(q, t)
            if cy > 0:
                edge = moved_x(q, HIGH)[t : t + 1]
                tile = jnp.where(
                    row == NY - 1, jnp.broadcast_to(edge, (NY, NX)), pltpu.roll(tile, NY - 1, 0)
                )
            elif cy < 0:
                edge = moved_x(q, LOW)[t : t + 1]
                tile = jnp.where(row == 0, jnp.broadcast_to(edge, (NY, NX)), pltpu.roll(tile, 1, 0))
            h.append(tile)
        density, flow = moments([pop[q, z] for q in range(Q)])
        back, by_porosity = pull_back(
            density, flow, h, por[z], kind[z].astype(jnp.float32), range(Q)
        )
        for q in range(Q):
            out[q, z] = back[q]
        sense[z] = sense[z] + by_porosity


VMEM = pl.BlockSpec(memory_space=pltpu.VMEM)
SMEM = pl.BlockSpec(memory_space=pltpu.SMEM)
HBM = pl.BlockSpec(memory_space=pltpu.HBM)


def call(kernel, shapes, specs, scratch=()):
    out = [
        shape if isinstance(shape, jax.ShapeDtypeStruct) else jax.ShapeDtypeStruct(shape, jnp.float32)
        for shape in shapes
    ]
    return pl.pallas_call(
        kernel,
        out_shape=out,
        in_specs=specs,
        out_specs=[VMEM] * len(out),
        scratch_shapes=list(scratch),
        compiler_params=pltpu.CompilerParams(vmem_limit_bytes=12 * 1024 * 1024),
    )


def both_ways(first, second, axis):
    count = lax.axis_size(axis)
    if axis in SWAPPED:
        one = [(i, i ^ 1) for i in range(count)]
        two = [((i + 1) % count, ((i ^ 1) + 1) % count) for i in range(count)]
    else:
        one = [(i, (i + 1) % count) for i in range(count)]
        two = [(t, s) for s, t in one]
    return lax.ppermute(first, axis, one), lax.ppermute(second, axis, two)


def on_device(populations, porosity, node_type, step_index, adjoint_end):
    tile = (NY, NX)
    moved, first, second, pop, adj, por, kind = call(
        collide_kernel,
        [(Q, NZ, *tile), (len(Z_UP), *tile), (len(Z_DOWN), *tile)]
        + [(Q, NZ, *tile), (Q, NZ, *tile), (NZ, *tile), jax.ShapeDtypeStruct((NZ, *tile), jnp.int32)],
        [SMEM] + [HBM] * 4,
        [pltpu.SemaphoreType.DMA((4,))],
    )(
        step_index,
        *(
            pltpu.with_memory_space_constraint(x, pltpu.HBM)
            for x in (populations, adjoint_end, porosity, node_type)
        ),
    )
    one, two = both_ways(first, second, "gz")
    shifted, up, down, *copies = call(
        rows_kernel if "gy" in SWAPPED else functools.partial(without_copies, rows_kernel),
        [(len(Y_FIELDS) * EXT * ROWS, NX), (Y_UP_ROWS, NX), (Y_DOWN_ROWS, NX)]
        + [(Y_UP_ROWS, NX), (Y_DOWN_ROWS, NX)] * ("gy" in SWAPPED),
        [VMEM] * 6,
    )(moved, adj, por, kind, one, two)
    first, second = copies or (up, down)
    one, two = both_ways(first, second, "gy")
    wide, packed = call(
        columns_kernel,
        [(len(X_FIELDS) * (EXT + 2) * ROWS, NX), (PACKED, *tile)],
        [VMEM] * 5,
    )(shifted, up, down, one, two)
    one, two = both_ways(packed, packed, "gx")
    adjoint, sense = call(
        adjoint_kernel,
        [(Q, NZ, *tile), (NZ, *tile)],
        [VMEM] * 7,
        [pltpu.VMEM((Q * (SIDES + 1) * ROWS, NX), jnp.float32)],
    )(wide, packed, one, two, pop, por, kind)
    return adjoint, sense


def without_copies(kernel, *refs):
    kernel(*refs, None, None)


def solution(mesh):
    brick = P(None, "gz", "gy", "gx")
    field = P("gz", "gy", "gx")
    return jax.shard_map(
        on_device,
        mesh=mesh,
        in_specs=(brick, field, field, P(), brick),
        out_specs=(brick, field),
        check_vma=False,
    )
```

```python
import functools
import math

import jax
import jax.numpy as jnp
from jax import lax
from jax.experimental import pallas as pl
from jax.experimental.pallas import tpu as pltpu
from jax.sharding import PartitionSpec as P

VELOCITIES = (
    (0, 0, 0),
    (1, 0, 0),
    (-1, 0, 0),
    (0, 1, 0),
    (0, -1, 0),
    (0, 0, 1),
    (0, 0, -1),
    (1, 1, 0),
    (-1, -1, 0),
    (1, -1, 0),
    (-1, 1, 0),
    (1, 0, 1),
    (-1, 0, -1),
    (1, 0, -1),
    (-1, 0, 1),
    (0, 1, 1),
    (0, -1, -1),
    (0, 1, -1),
    (0, -1, 1),
)
WEIGHTS = (1.0 / 3.0,) + (1.0 / 18.0,) * 6 + (1.0 / 36.0,) * 12
OPPOSITE = (0, 2, 1, 4, 3, 6, 5, 8, 7, 10, 9, 12, 11, 14, 13, 16, 15, 18, 17)
Q = 19
RATE = 1.25
RAMP = 0.1
NZ, NY, NX = 4, 8, 128
EXT = NZ + 2
LOW, HIGH = EXT, EXT + 1
SIDES = EXT + 2
ROWS = 8
SWAPPED = ("gx",)
REVERSED = ("gz",)

FLUID, WALL, INLET, OUTLET = -1, 0, 1, 2

FORWARD, ADJOINT, DESIGN, KIND = range(4)


def opposed(c):
    return tuple(-i for i in c)


Z_FIELDS = (
    [(FORWARD, q, VELOCITIES[q][2]) for q in range(Q)]
    + [(ADJOINT, q, -VELOCITIES[q][2]) for q in range(Q)]
    + [(DESIGN, 0, 0), (KIND, 0, 0)]
)
Z_UP, Z_DOWN = [], []
for _what, _which, _s in Z_FIELDS:
    if _s >= 0:
        Z_UP += [(_what, _which, p) for p in range(NZ - 1 - _s, NZ)]
    if _s <= 0:
        Z_DOWN += [(_what, _which, p) for p in range(0, 1 - _s)]
Z_UP_AT = {entry: i for i, entry in enumerate(Z_UP)}
Z_DOWN_AT = {entry: i for i, entry in enumerate(Z_DOWN)}

Y_FIELDS = []
for _cy in (-1, 0, 1):
    for _cx in (-1, 0, 1):
        _same = [q for q in range(Q) if VELOCITIES[q][:2] == (_cx, _cy)]
        Y_FIELDS.append((FORWARD, (_cx, _cy, 0), [(1, q) for q in _same], _cy))
        _deep = [(VELOCITIES[q][2], q) for q in _same if VELOCITIES[q][2]]
        if _deep:
            Y_FIELDS.append((FORWARD, (_cx, _cy, 1), _deep, _cy))
Y_FIELDS += [(ADJOINT, q, [(1, q)], -VELOCITIES[q][1]) for q in range(Q)]
Y_FIELDS += [(DESIGN, 0, [(1, 0)], 0), (KIND, 0, [(1, 0)], 0)]
Y_AT = {(what, which): i for i, (what, which, _, _) in enumerate(Y_FIELDS)}
Y_UP, Y_DOWN = [], []
for _i, (_, _, _, _s) in enumerate(Y_FIELDS):
    if _s >= 0:
        Y_UP += [(_i, row) for row in range(NY - 1 - _s, NY)]
    if _s <= 0:
        Y_DOWN += [(_i, row) for row in range(0, 1 - _s)]
Y_UP_AT = {entry: i for i, entry in enumerate(Y_UP)}
Y_DOWN_AT = {entry: i for i, entry in enumerate(Y_DOWN)}


def padded(rows):
    return -(-(rows + 2) // ROWS) * ROWS


Y_UP_ROWS, Y_DOWN_ROWS = padded(len(Y_UP) * EXT), padded(len(Y_DOWN) * EXT)

X_FIELDS = []
for _s in (1, -1, 0):
    X_FIELDS += [(FORWARD, (_s, i)) for i in range(3)]
    X_FIELDS += [(ADJOINT, q) for q in range(Q) if -VELOCITIES[q][0] == _s]
X_FIELDS += [(DESIGN, 0), (KIND, 0)]
X_AT = {entry: i for i, entry in enumerate(X_FIELDS)}
PER_TILE = 4
PACKED = -(-len(X_FIELDS) // PER_TILE)


def shift_of(entry):
    what, which = entry
    if what == FORWARD:
        return which[0]
    return -VELOCITIES[which][0] if what == ADJOINT else 0


def add_up(terms):
    total = None
    for sign, value in terms:
        if total is None:
            total = value if sign > 0 else -value
        else:
            total = total + value if sign > 0 else total - value
    return total


def moments(f):
    density = add_up([(1, f[q]) for q in range(Q)])
    flow = [
        add_up([(VELOCITIES[q][i], f[q]) for q in range(Q) if VELOCITIES[q][i]])
        for i in range(3)
    ]
    return density, flow


def along(q, vector):
    return add_up([(VELOCITIES[q][i], vector[i]) for i in range(3) if VELOCITIES[q][i]])


def collide(f, porosity, kinds, speed):
    density, flow = moments(f)
    inverse = 1.0 / density
    fluid = kinds == FLUID
    wall = kinds == WALL
    inlet = kinds == INLET
    damping = RAMP * (1.0 - porosity) / (RAMP + porosity)
    kept = jnp.where(fluid, 1.0 - damping, 1.0)
    v = [
        jnp.where(inlet, speed if i == 0 else 0.0, flow[i] * inverse * kept)
        for i in range(3)
    ]
    r = jnp.where(inlet, 1.0, density)
    scale = jnp.where(fluid, RATE, 1.0) * r
    keep = jnp.where(fluid, 1.0 - RATE, 0.0)
    base = 1.0 - 1.5 * (v[0] * v[0] + v[1] * v[1] + v[2] * v[2])
    out = []
    for q in range(Q):
        p = along(q, v)
        shape = base if p is None else base + p * (3.0 + 4.5 * p)
        moved = keep * f[q] + (WEIGHTS[q] * scale) * shape
        out.append(jnp.where(wall, f[OPPOSITE[q]], moved))
    return out


def prepare(density, flow, porosity, kinds):
    inverse = 1.0 / density
    return [density, *(flow[i] * inverse for i in range(3)), 1.0 / (RAMP + porosity)]


def pull_back(state, h, porosity, kinds, wanted):
    density, *u, ramp = state
    fluid = kinds == FLUID
    wall = kinds == WALL
    outlet = kinds == OUTLET
    square = u[0] * u[0] + u[1] * u[1] + u[2] * u[2]
    damping = jnp.where(fluid, RAMP * (1.0 - porosity) * ramp, 0.0)
    kept = 1.0 - damping
    v = [kept * u[i] for i in range(3)]
    face, edge = WEIGHTS[1], WEIGHTS[7]
    plus = {}
    minus = {}
    for q in range(1, Q, 2):
        plus[q] = h[q] + h[q + 1]
        minus[q] = h[q] - h[q + 1]
    xy, yx, xz, zx, yz, zy = (plus[q] for q in (7, 9, 11, 13, 15, 17))
    second = [
        [face * plus[1] + edge * ((xy + yx) + (xz + zx)), edge * (xy - yx), edge * (xz - zx)],
        [None, face * plus[3] + edge * ((xy + yx) + (yz + zy)), edge * (yz - zy)],
        [None, None, face * plus[5] + edge * ((xz + zx) + (yz + zy))],
    ]
    second[1][0], second[2][0], second[2][1] = second[0][1], second[0][2], second[1][2]
    zero = (
        WEIGHTS[0] * h[0]
        + face * (plus[1] + plus[3] + plus[5])
        + edge * ((xy + yx) + (xz + zx) + (yz + zy))
    )
    first = [
        face * minus[1] + edge * ((minus[7] + minus[9]) + (minus[11] + minus[13])),
        face * minus[3] + edge * ((minus[7] - minus[9]) + (minus[15] + minus[17])),
        face * minus[5] + edge * ((minus[11] - minus[13]) + (minus[15] - minus[17])),
    ]
    bent = [
        4.5 * (second[i][0] * v[0] + second[i][1] * v[1] + second[i][2] * v[2])
        - 1.5 * zero * v[i]
        for i in range(3)
    ]
    level = zero + sum(v[i] * (3.0 * first[i] + bent[i]) for i in range(3))
    slope = [3.0 * first[i] + 2.0 * bent[i] for i in range(3)]
    rate = jnp.where(fluid, RATE, jnp.where(outlet, 1.0, 0.0))
    keep = jnp.where(fluid, 1.0 - RATE, 0.0)
    turn = sum(slope[i] * u[i] for i in range(3))
    moved_rate = rate * kept
    tilt = [moved_rate * slope[i] + 2.0 * damping * u[i] for i in range(3)]
    flat = rate * level - moved_rate * turn - damping * square
    out = {}
    for q in wanted:
        p = along(q, tilt)
        moved = keep * h[q] + (flat if p is None else flat + p)
        out[q] = jnp.where(wall, h[OPPOSITE[q]], moved)
    by_porosity = jnp.where(
        fluid,
        (-RAMP * (1.0 + RAMP)) * ramp * ramp * density * (square - RATE * turn),
        0.0,
    )
    return out, by_porosity


def by_side(axis, act, first, second):
    if axis in REVERSED:
        first, second = second, first
    if axis not in SWAPPED:
        act(first, second)
        return
    here = lax.rem(lax.axis_index(axis), 2)

    @pl.when(here == 0)
    def _():
        act(first, second)

    @pl.when(here == 1)
    def _():
        act(second, first)


def from_side(axis, first, second):
    if axis in REVERSED:
        first, second = second, first
    if axis not in SWAPPED:
        return (lambda at: first[at]), (lambda at: second[at])
    even = lax.rem(lax.axis_index(axis), 2) == 0
    return (
        lambda at: jnp.where(even, second[at], first[at]),
        lambda at: jnp.where(even, first[at], second[at]),
    )


def collide_kernel(
    step, pop_hbm, adj_hbm, por_hbm, kind_hbm, moved, first, second, pop, adj, por, kind, raw, done
):
    copies = [
        pltpu.make_async_copy(source, target, done.at[i])
        for i, (source, target) in enumerate(
            ((pop_hbm, pop), (por_hbm, por), (kind_hbm, raw), (adj_hbm, adj))
        )
    ]
    for copy in copies:
        copy.start()
    moment = jnp.full((NY, NX), step[0] & 63, jnp.int32).astype(jnp.float32)
    speed = 0.1 * (1.0 + 0.8 * jnp.sin((2.0 * math.pi / 64.0) * moment))
    for copy in copies[:3]:
        copy.wait()
    for z in range(NZ):
        kind[z] = (raw[z] - 1).astype(jnp.float32)
        collided = collide([pop[q, z] for q in range(Q)], por[z], kind[z], speed)
        for q in range(Q):
            moved[q, z] = collided[q]
    copies[3].wait()

    def value(what, which, z):
        if what == FORWARD:
            return moved[which, z]
        if what == ADJOINT:
            return adj[which, z]
        return por[z] if what == DESIGN else kind[z]

    def write(up, down):
        for table, out in ((Z_UP_AT, up), (Z_DOWN_AT, down)):
            for entry, at in table.items():
                out[at] = value(*entry)

    by_side("gz", write, first, second)


def copy_both(up, down, first, second):
    for i in range(up.shape[0] // ROWS):
        rows = pl.ds(i * ROWS, ROWS)
        first[rows, :] = up[rows, :]
        second[rows, :] = down[rows, :]


def rows_kernel(moved, adj, por, kind, one, two, shifted, up, down, first, second):
    below, above = from_side("gz", one, two)

    def plane_of(what, which, z):
        if z < 0:
            return below(Z_UP_AT[what, which, z + NZ])
        if z >= NZ:
            return above(Z_DOWN_AT[what, which, z - NZ])
        if what == FORWARD:
            return moved[which, z]
        if what == ADJOINT:
            return adj[which, z]
        return por[z] if what == DESIGN else kind[z]

    for i, (what, _, parts, _) in enumerate(Y_FIELDS):
        for t in range(EXT):
            terms = []
            for sign, q in parts:
                s = VELOCITIES[q][2] if what == FORWARD else 0
                if what == ADJOINT:
                    s = -VELOCITIES[q][2]
                terms.append((sign, plane_of(what, q, t - 1 - s)))
            shifted[pl.ds((i * EXT + t) * ROWS, ROWS), :] = add_up(terms)
    def write(forward, backward):
        for table, out in ((Y_UP, forward), (Y_DOWN, backward)):
            for at, (i, row) in enumerate(table):
                out[pl.ds(at * EXT, EXT), :] = shifted[
                    pl.ds(i * EXT * ROWS + row, EXT, stride=ROWS), :
                ]
            used = len(table) * EXT
            out[pl.ds(used, out.shape[0] - used), :] = jnp.zeros(
                (out.shape[0] - used, NX), jnp.float32
            )

    write(up, down)
    if "gy" in SWAPPED:
        by_side("gy", functools.partial(copy_both, up, down), first, second)


def columns_kernel(shifted, up, down, one, two, wide, packed):
    left, right = from_side("gy", one, two)
    row = lax.broadcasted_iota(jnp.int32, (NY, NX), 0)
    lane = lax.broadcasted_iota(jnp.int32, (NY, NX), 1)

    def rows_of(ref, at):
        rows = (pl.ds(at * EXT, ROWS), slice(None))
        return ref(rows) if callable(ref) else ref[rows]

    def row_of(ref, at, t):
        return jnp.broadcast_to(ref((pl.ds(at * EXT + t, 1), slice(None))), (NY, NX))

    def tile_of(entry, t):
        i = Y_AT[entry]
        s = Y_FIELDS[i][3]
        if t == LOW:
            if s < 0:
                return rows_of(down, Y_DOWN_AT[i, 0])
            return rows_of(left, Y_UP_AT[i, NY - 1 - s])
        if t == HIGH:
            if s > 0:
                return rows_of(up, Y_UP_AT[i, NY - 1])
            return rows_of(right, Y_DOWN_AT[i, -s])
        own = shifted[pl.ds((i * EXT + t) * ROWS, ROWS), :]
        if s > 0:
            return jnp.where(
                row == 0, row_of(left, Y_UP_AT[i, NY - 1], t), pltpu.roll(own, 1, 0)
            )
        if s < 0:
            return jnp.where(
                row == NY - 1, row_of(right, Y_DOWN_AT[i, 0], t), pltpu.roll(own, NY - 1, 0)
            )
        return own

    for u in range(PACKED):
        total = None
        for j, entry in enumerate(X_FIELDS[u * PER_TILE : (u + 1) * PER_TILE]):
            f = u * PER_TILE + j
            what, which = entry
            for t in range(EXT + 2):
                if what != FORWARD:
                    tile = tile_of(entry, t)
                else:
                    cx, part = which
                    terms = []
                    for cy in (-1, 0, 1):
                        source = (FORWARD, (cx, cy, 1 if part == 2 else 0))
                        if source in Y_AT and (part != 1 or cy):
                            sign = cy if part == 1 else 1
                            terms.append((sign, tile_of(source, t)))
                    tile = add_up(terms)
                wide[pl.ds((f * (EXT + 2) + t) * ROWS, ROWS), :] = tile
                k = j * (EXT + 2) + t
                turned = pltpu.roll(tile, (2 + 4 * k) % NX, 1)
                total = turned if total is None else jnp.where(lane >= 4 * k, turned, total)
        packed[u] = total


STATE = 5


def wanted_at(t):
    if t == SIDES:
        return list(range(Q))
    if t in (LOW, HIGH):
        return [q for q in range(Q) if VELOCITIES[q][1] == (1 if t == HIGH else -1)]
    if t in (0, EXT - 1):
        return [q for q in range(Q) if VELOCITIES[q][2] == (1 if t else -1)]
    return list(range(Q))


def later_adjoint(value):
    parts = {s: [value((FORWARD, (s, i))) for i in range(3)] for s in (-1, 0, 1)}
    density = parts[0][0] + parts[1][0] + parts[-1][0]
    flow = [
        parts[1][0] - parts[-1][0],
        parts[0][1] + parts[1][1] + parts[-1][1],
        parts[0][2] + parts[1][2] + parts[-1][2],
    ]
    h = [value((ADJOINT, q)) for q in range(Q)]
    design, kinds = value((DESIGN, 0)), value((KIND, 0))
    return prepare(density, flow, design, kinds), h, design, kinds


def at(q, t):
    return pl.ds((q * (SIDES + 1) + t) * ROWS, ROWS)


def inner_kernel(wide, pop, por, kind, states, sense, ready):
    for t in range(SIDES):

        def value(entry, t=t):
            own = wide[pl.ds((X_AT[entry] * (EXT + 2) + t) * ROWS, ROWS), :]
            s = shift_of(entry)
            return pltpu.roll(own, s % NX, 1) if s else own

        back, by_porosity = pull_back(*later_adjoint(value), wanted_at(t))
        for q in wanted_at(t):
            states[at(q, t), :] = back[q]
        if 1 <= t <= NZ:
            sense[t - 1] = by_porosity
    for z in range(NZ):
        density, flow = moments([pop[q, z] for q in range(Q)])
        for i, part in enumerate(prepare(density, flow, por[z], kind[z])):
            ready[i, z] = part


def adjoint_kernel(states, sense, ready, packed, one, two, por, kind, out_hbm, sense_hbm, out, sum_, sides, done):
    lane = lax.broadcasted_iota(jnp.int32, (NY, NX), 1)
    row = lax.broadcasted_iota(jnp.int32, (NY, NX), 0)
    before, after = from_side("gx", one, two)
    slot = lane & 3
    ends = []
    for u in range(PACKED):
        s = shift_of(X_FIELDS[u * PER_TILE])
        own = packed[u]
        if s > 0:
            ends.append(jnp.where(slot < 2, own, pltpu.roll(before(u), 2, 1)))
        elif s < 0:
            ends.append(jnp.where(slot < 2, pltpu.roll(after(u), NX - 2, 1), own))
        else:
            here = jnp.where(slot == 1, own, after(u))
            there = jnp.where(slot == 1, before(u), own)
            ends.append(
                jnp.where(slot < 2, pltpu.roll(here, NX - 1, 1), pltpu.roll(there, 1, 1))
            )

    def value(entry):
        u, j = divmod(X_AT[entry], PER_TILE)
        return pltpu.roll(ends[u], NX - 32 * j, 1) if j else ends[u]

    def together(tile):
        return jnp.where(slot == 0, tile, pltpu.roll(tile, NX - 2, 1))

    back, by_porosity = pull_back(*later_adjoint(value), wanted_at(SIDES))
    for q in range(Q):
        sides[q] = back[q] if VELOCITIES[q][0] else together(back[q])
    by_porosity = together(by_porosity)
    last, first_two, last_two = lane == NX - 1, lane < 2, lane >= NX - 2
    outer = (lane == 0) | last

    def moved_x(q, t):
        tile = states[at(q, t), :]
        cx = VELOCITIES[q][0]
        if cx > 0:
            turned = pltpu.roll(sides[q], NX - 2 - 4 * t, 1)
            return jnp.where(last_two, turned, pltpu.roll(tile, NX - 1, 1))
        if cx < 0:
            turned = pltpu.roll(sides[q], NX - 2 - 4 * t, 1)
            return jnp.where(first_two, turned, pltpu.roll(tile, 1, 1))
        return jnp.where(outer, pltpu.roll(sides[q], NX - 1 - 4 * t, 1), tile)

    copies = []
    for z in range(NZ):
        h = []
        for q in range(Q):
            _, cy, cz = VELOCITIES[q]
            t = z + cz + 1
            tile = moved_x(q, t)
            if cy:
                edge = moved_x(q, HIGH if cy > 0 else LOW)[t : t + 1]
                tile = jnp.where(
                    row == (NY - 1 if cy > 0 else 0),
                    jnp.broadcast_to(edge, (NY, NX)),
                    pltpu.roll(tile, NY - 1 if cy > 0 else 1, 0),
                )
            h.append(tile)
        back, now = pull_back(
            [ready[i, z] for i in range(STATE)], h, por[z], kind[z], range(Q)
        )
        for q in range(Q):
            out[z, q] = back[q]
        copies.append(pltpu.make_async_copy(out.at[z], out_hbm.at[:, z], done.at[z]))
        copies[-1].start()
        then = jnp.where(outer, pltpu.roll(by_porosity, NX - 1 - 4 * (z + 1), 1), sense[z])
        sum_[z] = then + now
    copies.append(pltpu.make_async_copy(sum_, sense_hbm, done.at[NZ]))
    copies[-1].start()
    for copy in copies:
        copy.wait()


VMEM = pl.BlockSpec(memory_space=pltpu.VMEM)
SMEM = pl.BlockSpec(memory_space=pltpu.SMEM)
HBM = pl.BlockSpec(memory_space=pltpu.HBM)


def call(kernel, shapes, specs, scratch=(), out_specs=None, cost=None):
    out = [
        shape if isinstance(shape, jax.ShapeDtypeStruct) else jax.ShapeDtypeStruct(shape, jnp.float32)
        for shape in shapes
    ]
    return pl.pallas_call(
        kernel,
        out_shape=out,
        in_specs=specs,
        out_specs=out_specs or [VMEM] * len(out),
        scratch_shapes=list(scratch),
        cost_estimate=cost,
        compiler_params=pltpu.CompilerParams(vmem_limit_bytes=12 * 1024 * 1024),
    )


def both_ways(first, second, axis):
    count = lax.axis_size(axis)
    if axis in SWAPPED:
        one = [(i, i ^ 1) for i in range(count)]
        two = [((i + 1) % count, ((i ^ 1) + 1) % count) for i in range(count)]
    else:
        one = [(i, i + 1) for i in range(count - 1)]
        two = [(t, s) for s, t in one]
    if axis != "gx":
        two = [(s, t) for s, t in two if abs(s - t) == 1]
    if axis in REVERSED:
        one, two = two, one
    return lax.ppermute(first, axis, one), lax.ppermute(second, axis, two)


def on_device(populations, porosity, node_type, step_index, adjoint_end):
    tile = (NY, NX)
    moved, first, second, pop, adj, por, kind = call(
        collide_kernel,
        [(Q, NZ, *tile), (len(Z_UP), *tile), (len(Z_DOWN), *tile)]
        + [(Q, NZ, *tile), (Q, NZ, *tile), (NZ, *tile), (NZ, *tile)],
        [SMEM] + [HBM] * 4,
        [pltpu.VMEM((NZ, *tile), jnp.int32), pltpu.SemaphoreType.DMA((4,))],
    )(
        step_index,
        *(
            pltpu.with_memory_space_constraint(x, pltpu.HBM)
            for x in (populations, adjoint_end, porosity, node_type)
        ),
    )
    one, two = both_ways(first, second, "gz")
    shifted, up, down, *copies = call(
        rows_kernel if "gy" in SWAPPED else functools.partial(without_copies, rows_kernel),
        [(len(Y_FIELDS) * EXT * ROWS, NX), (Y_UP_ROWS, NX), (Y_DOWN_ROWS, NX)]
        + [(Y_UP_ROWS, NX), (Y_DOWN_ROWS, NX)] * ("gy" in SWAPPED),
        [VMEM] * 6,
    )(moved, adj, por, kind, one, two)
    first, second = copies or (up, down)
    if "gy" in REVERSED and not copies:
        first, second = down, up
    one, two = both_ways(first, second, "gy")
    wide, packed = call(
        columns_kernel,
        [(len(X_FIELDS) * (EXT + 2) * ROWS, NX), (PACKED, *tile)],
        [VMEM] * 5,
    )(shifted, up, down, one, two)
    one, two = both_ways(packed, packed, "gx")
    states, part, ready = call(
        inner_kernel,
        [(Q * (SIDES + 1) * ROWS, NX), (NZ, *tile), (STATE, NZ, *tile)],
        [VMEM] * 4,
        cost=pl.CostEstimate(flops=20_000_000, bytes_accessed=4_000_000, transcendentals=0),
    )(wide, pop, por, kind)
    adjoint, sense = call(
        adjoint_kernel,
        [(Q, NZ, *tile), (NZ, *tile)],
        [VMEM] * 8,
        [
            pltpu.VMEM((NZ, Q, *tile), jnp.float32),
            pltpu.VMEM((NZ, *tile), jnp.float32),
            pltpu.VMEM((Q, *tile), jnp.float32),
            pltpu.SemaphoreType.DMA((NZ + 1,)),
        ],
        out_specs=[HBM] * 2,
    )(states, part, ready, packed, one, two, por, kind)
    return adjoint, sense


def without_copies(kernel, *refs):
    kernel(*refs, None, None)


def solution(mesh):
    brick = P(None, "gz", "gy", "gx")
    field = P("gz", "gy", "gx")
    return jax.shard_map(
        on_device,
        mesh=mesh,
        in_specs=(brick, field, field, P(), brick),
        out_specs=(brick, field),
        check_vma=False,
    )
```

```python
import functools
import math

import jax
import jax.numpy as jnp
from jax import lax
from jax.experimental import pallas as pl
from jax.experimental.pallas import tpu as pltpu
from jax.sharding import PartitionSpec as P

VELOCITIES = (
    (0, 0, 0),
    (1, 0, 0),
    (-1, 0, 0),
    (0, 1, 0),
    (0, -1, 0),
    (0, 0, 1),
    (0, 0, -1),
    (1, 1, 0),
    (-1, -1, 0),
    (1, -1, 0),
    (-1, 1, 0),
    (1, 0, 1),
    (-1, 0, -1),
    (1, 0, -1),
    (-1, 0, 1),
    (0, 1, 1),
    (0, -1, -1),
    (0, 1, -1),
    (0, -1, 1),
)
WEIGHTS = (1.0 / 3.0,) + (1.0 / 18.0,) * 6 + (1.0 / 36.0,) * 12
OPPOSITE = (0, 2, 1, 4, 3, 6, 5, 8, 7, 10, 9, 12, 11, 14, 13, 16, 15, 18, 17)
Q = 19
RATE = 1.25
RAMP = 0.1
NZ, NY, NX = 4, 8, 128
EXT = NZ + 2
LOW, HIGH = EXT, EXT + 1
SIDES = EXT + 2
ROWS = 8
SWAPPED = ("gx",)
REVERSED = ("gz",)

FLUID, WALL, INLET, OUTLET = -1, 0, 1, 2

FORWARD, ADJOINT, DESIGN, KIND = range(4)


def opposed(c):
    return tuple(-i for i in c)


Z_FIELDS = (
    [(FORWARD, q, VELOCITIES[q][2]) for q in range(Q)]
    + [(ADJOINT, q, -VELOCITIES[q][2]) for q in range(Q)]
    + [(DESIGN, 0, 0), (KIND, 0, 0)]
)
Z_UP, Z_DOWN = [], []
for _what, _which, _s in Z_FIELDS:
    if _s >= 0:
        Z_UP += [(_what, _which, p) for p in range(NZ - 1 - _s, NZ)]
    if _s <= 0:
        Z_DOWN += [(_what, _which, p) for p in range(0, 1 - _s)]
Z_UP_AT = {entry: i for i, entry in enumerate(Z_UP)}
Z_DOWN_AT = {entry: i for i, entry in enumerate(Z_DOWN)}

Y_FIELDS = []
for _cy in (-1, 0, 1):
    for _cx in (-1, 0, 1):
        _same = [q for q in range(Q) if VELOCITIES[q][:2] == (_cx, _cy)]
        Y_FIELDS.append((FORWARD, (_cx, _cy, 0), [(1, q) for q in _same], _cy))
        _deep = [(VELOCITIES[q][2], q) for q in _same if VELOCITIES[q][2]]
        if _deep:
            Y_FIELDS.append((FORWARD, (_cx, _cy, 1), _deep, _cy))
Y_FIELDS += [(ADJOINT, q, [(1, q)], -VELOCITIES[q][1]) for q in range(Q)]
Y_FIELDS += [(DESIGN, 0, [(1, 0)], 0), (KIND, 0, [(1, 0)], 0)]
Y_AT = {(what, which): i for i, (what, which, _, _) in enumerate(Y_FIELDS)}
Y_UP, Y_DOWN = [], []
for _i, (_, _, _, _s) in enumerate(Y_FIELDS):
    if _s >= 0:
        Y_UP += [(_i, row) for row in range(NY - 1 - _s, NY)]
    if _s <= 0:
        Y_DOWN += [(_i, row) for row in range(0, 1 - _s)]
Y_UP_AT = {entry: i for i, entry in enumerate(Y_UP)}
Y_DOWN_AT = {entry: i for i, entry in enumerate(Y_DOWN)}


def padded(rows):
    return -(-(rows + 2) // ROWS) * ROWS


Y_UP_ROWS, Y_DOWN_ROWS = padded(len(Y_UP) * EXT), padded(len(Y_DOWN) * EXT)

X_FIELDS = []
for _s in (1, -1, 0):
    X_FIELDS += [(FORWARD, (_s, i)) for i in range(3)]
    X_FIELDS += [(ADJOINT, q) for q in range(Q) if -VELOCITIES[q][0] == _s]
X_FIELDS += [(DESIGN, 0), (KIND, 0)]
X_AT = {entry: i for i, entry in enumerate(X_FIELDS)}
PER_TILE = 4
PACKED = -(-len(X_FIELDS) // PER_TILE)


def shift_of(entry):
    what, which = entry
    if what == FORWARD:
        return which[0]
    return -VELOCITIES[which][0] if what == ADJOINT else 0


def add_up(terms):
    total = None
    for sign, value in terms:
        if total is None:
            total = value if sign > 0 else -value
        else:
            total = total + value if sign > 0 else total - value
    return total


def moments(f):
    density = add_up([(1, f[q]) for q in range(Q)])
    flow = [
        add_up([(VELOCITIES[q][i], f[q]) for q in range(Q) if VELOCITIES[q][i]])
        for i in range(3)
    ]
    return density, flow


def along(q, vector):
    return add_up([(VELOCITIES[q][i], vector[i]) for i in range(3) if VELOCITIES[q][i]])


def collide(f, porosity, kinds, speed):
    density, flow = moments(f)
    inverse = 1.0 / density
    fluid = kinds == FLUID
    wall = kinds == WALL
    inlet = kinds == INLET
    damping = RAMP * (1.0 - porosity) / (RAMP + porosity)
    kept = jnp.where(fluid, 1.0 - damping, 1.0)
    v = [
        jnp.where(inlet, speed if i == 0 else 0.0, flow[i] * inverse * kept)
        for i in range(3)
    ]
    r = jnp.where(inlet, 1.0, density)
    scale = jnp.where(fluid, RATE, 1.0) * r
    keep = jnp.where(fluid, 1.0 - RATE, 0.0)
    base = 1.0 - 1.5 * (v[0] * v[0] + v[1] * v[1] + v[2] * v[2])
    out = []
    for q in range(Q):
        p = along(q, v)
        shape = base if p is None else base + p * (3.0 + 4.5 * p)
        moved = keep * f[q] + (WEIGHTS[q] * scale) * shape
        out.append(jnp.where(wall, f[OPPOSITE[q]], moved))
    return out


def prepare(density, flow, porosity, kinds):
    inverse = 1.0 / density
    return [density, *(flow[i] * inverse for i in range(3)), 1.0 / (RAMP + porosity)]


def pull_back(state, h, porosity, kinds, wanted):
    density, *u, ramp = state
    fluid = kinds == FLUID
    wall = kinds == WALL
    outlet = kinds == OUTLET
    square = u[0] * u[0] + u[1] * u[1] + u[2] * u[2]
    damping = jnp.where(fluid, RAMP * (1.0 - porosity) * ramp, 0.0)
    kept = 1.0 - damping
    v = [kept * u[i] for i in range(3)]
    face, edge = WEIGHTS[1], WEIGHTS[7]
    plus = {}
    minus = {}
    for q in range(1, Q, 2):
        plus[q] = h[q] + h[q + 1]
        minus[q] = h[q] - h[q + 1]
    xy, yx, xz, zx, yz, zy = (plus[q] for q in (7, 9, 11, 13, 15, 17))
    second = [
        [face * plus[1] + edge * ((xy + yx) + (xz + zx)), edge * (xy - yx), edge * (xz - zx)],
        [None, face * plus[3] + edge * ((xy + yx) + (yz + zy)), edge * (yz - zy)],
        [None, None, face * plus[5] + edge * ((xz + zx) + (yz + zy))],
    ]
    second[1][0], second[2][0], second[2][1] = second[0][1], second[0][2], second[1][2]
    zero = (
        WEIGHTS[0] * h[0]
        + face * (plus[1] + plus[3] + plus[5])
        + edge * ((xy + yx) + (xz + zx) + (yz + zy))
    )
    first = [
        face * minus[1] + edge * ((minus[7] + minus[9]) + (minus[11] + minus[13])),
        face * minus[3] + edge * ((minus[7] - minus[9]) + (minus[15] + minus[17])),
        face * minus[5] + edge * ((minus[11] - minus[13]) + (minus[15] - minus[17])),
    ]
    bent = [
        4.5 * (second[i][0] * v[0] + second[i][1] * v[1] + second[i][2] * v[2])
        - 1.5 * zero * v[i]
        for i in range(3)
    ]
    level = zero + sum(v[i] * (3.0 * first[i] + bent[i]) for i in range(3))
    slope = [3.0 * first[i] + 2.0 * bent[i] for i in range(3)]
    rate = jnp.where(fluid, RATE, jnp.where(outlet, 1.0, 0.0))
    keep = jnp.where(fluid, 1.0 - RATE, 0.0)
    turn = sum(slope[i] * u[i] for i in range(3))
    moved_rate = rate * kept
    tilt = [moved_rate * slope[i] + 2.0 * damping * u[i] for i in range(3)]
    flat = rate * level - moved_rate * turn - damping * square
    out = {}
    for q in wanted:
        p = along(q, tilt)
        moved = keep * h[q] + (flat if p is None else flat + p)
        out[q] = jnp.where(wall, h[OPPOSITE[q]], moved)
    by_porosity = jnp.where(
        fluid,
        (-RAMP * (1.0 + RAMP)) * ramp * ramp * density * (square - RATE * turn),
        0.0,
    )
    return out, by_porosity


def by_side(axis, act, first, second):
    if axis in REVERSED:
        first, second = second, first
    if axis not in SWAPPED:
        act(first, second)
        return
    here = lax.rem(lax.axis_index(axis), 2)

    @pl.when(here == 0)
    def _():
        act(first, second)

    @pl.when(here == 1)
    def _():
        act(second, first)


def from_side(axis, first, second):
    if axis in REVERSED:
        first, second = second, first
    if axis not in SWAPPED:
        return (lambda at: first[at]), (lambda at: second[at])
    even = lax.rem(lax.axis_index(axis), 2) == 0
    return (
        lambda at: jnp.where(even, second[at], first[at]),
        lambda at: jnp.where(even, first[at], second[at]),
    )


def collide_kernel(
    step, pop_hbm, adj_hbm, por_hbm, kind_hbm, moved, first, second, pop, adj, por, kind, raw, done
):
    copies = [
        pltpu.make_async_copy(source, target, done.at[i])
        for i, (source, target) in enumerate(
            ((pop_hbm, pop), (por_hbm, por), (kind_hbm, raw), (adj_hbm, adj))
        )
    ]
    for copy in copies:
        copy.start()
    moment = jnp.full((NY, NX), step[0] & 63, jnp.int32).astype(jnp.float32)
    speed = 0.1 * (1.0 + 0.8 * jnp.sin((2.0 * math.pi / 64.0) * moment))
    for copy in copies[:3]:
        copy.wait()
    for z in range(NZ):
        kind[z] = (raw[z] - 1).astype(jnp.float32)
        collided = collide([pop[q, z] for q in range(Q)], por[z], kind[z], speed)
        for q in range(Q):
            moved[q, z] = collided[q]
    copies[3].wait()

    def value(what, which, z):
        if what == FORWARD:
            return moved[which, z]
        if what == ADJOINT:
            return adj[which, z]
        return por[z] if what == DESIGN else kind[z]

    def write(up, down):
        for table, out in ((Z_UP_AT, up), (Z_DOWN_AT, down)):
            for entry, at in table.items():
                out[at] = value(*entry)

    by_side("gz", write, first, second)


def copy_both(up, down, first, second):
    for i in range(up.shape[0] // ROWS):
        rows = pl.ds(i * ROWS, ROWS)
        first[rows, :] = up[rows, :]
        second[rows, :] = down[rows, :]


def rows_kernel(moved, adj, por, kind, one, two, shifted, up, down, first, second):
    below, above = from_side("gz", one, two)

    def plane_of(what, which, z):
        if z < 0:
            return below(Z_UP_AT[what, which, z + NZ])
        if z >= NZ:
            return above(Z_DOWN_AT[what, which, z - NZ])
        if what == FORWARD:
            return moved[which, z]
        if what == ADJOINT:
            return adj[which, z]
        return por[z] if what == DESIGN else kind[z]

    for i, (what, _, parts, _) in enumerate(Y_FIELDS):
        for t in range(EXT):
            terms = []
            for sign, q in parts:
                s = VELOCITIES[q][2] if what == FORWARD else 0
                if what == ADJOINT:
                    s = -VELOCITIES[q][2]
                terms.append((sign, plane_of(what, q, t - 1 - s)))
            shifted[pl.ds((i * EXT + t) * ROWS, ROWS), :] = add_up(terms)
    def write(forward, backward):
        for table, out in ((Y_UP, forward), (Y_DOWN, backward)):
            for at, (i, row) in enumerate(table):
                out[pl.ds(at * EXT, EXT), :] = shifted[
                    pl.ds(i * EXT * ROWS + row, EXT, stride=ROWS), :
                ]
            used = len(table) * EXT
            out[pl.ds(used, out.shape[0] - used), :] = jnp.zeros(
                (out.shape[0] - used, NX), jnp.float32
            )

    write(up, down)
    if "gy" in SWAPPED:
        by_side("gy", functools.partial(copy_both, up, down), first, second)


def columns_kernel(shifted, up, down, one, two, wide, packed):
    left, right = from_side("gy", one, two)
    row = lax.broadcasted_iota(jnp.int32, (NY, NX), 0)
    lane = lax.broadcasted_iota(jnp.int32, (NY, NX), 1)

    def rows_of(ref, at):
        rows = (pl.ds(at * EXT, ROWS), slice(None))
        return ref(rows) if callable(ref) else ref[rows]

    def row_of(ref, at, t):
        return jnp.broadcast_to(ref((pl.ds(at * EXT + t, 1), slice(None))), (NY, NX))

    def tile_of(entry, t):
        i = Y_AT[entry]
        s = Y_FIELDS[i][3]
        if t == LOW:
            if s < 0:
                return rows_of(down, Y_DOWN_AT[i, 0])
            return rows_of(left, Y_UP_AT[i, NY - 1 - s])
        if t == HIGH:
            if s > 0:
                return rows_of(up, Y_UP_AT[i, NY - 1])
            return rows_of(right, Y_DOWN_AT[i, -s])
        own = shifted[pl.ds((i * EXT + t) * ROWS, ROWS), :]
        if s > 0:
            return jnp.where(
                row == 0, row_of(left, Y_UP_AT[i, NY - 1], t), pltpu.roll(own, 1, 0)
            )
        if s < 0:
            return jnp.where(
                row == NY - 1, row_of(right, Y_DOWN_AT[i, 0], t), pltpu.roll(own, NY - 1, 0)
            )
        return own

    for u in range(PACKED):
        total = None
        for j, entry in enumerate(X_FIELDS[u * PER_TILE : (u + 1) * PER_TILE]):
            f = u * PER_TILE + j
            what, which = entry
            for t in range(EXT + 2):
                if what != FORWARD:
                    tile = tile_of(entry, t)
                else:
                    cx, part = which
                    terms = []
                    for cy in (-1, 0, 1):
                        source = (FORWARD, (cx, cy, 1 if part == 2 else 0))
                        if source in Y_AT and (part != 1 or cy):
                            sign = cy if part == 1 else 1
                            terms.append((sign, tile_of(source, t)))
                    tile = add_up(terms)
                wide[pl.ds((f * (EXT + 2) + t) * ROWS, ROWS), :] = tile
                k = j * (EXT + 2) + t
                turned = pltpu.roll(tile, (2 + 4 * k) % NX, 1)
                total = turned if total is None else jnp.where(lane >= 4 * k, turned, total)
        packed[u] = total


STATE = 5


def wanted_at(t):
    if t == SIDES:
        return list(range(Q))
    if t in (LOW, HIGH):
        return [q for q in range(Q) if VELOCITIES[q][1] == (1 if t == HIGH else -1)]
    if t in (0, EXT - 1):
        return [q for q in range(Q) if VELOCITIES[q][2] == (1 if t else -1)]
    return list(range(Q))


def later_adjoint(value):
    parts = {s: [value((FORWARD, (s, i))) for i in range(3)] for s in (-1, 0, 1)}
    density = parts[0][0] + parts[1][0] + parts[-1][0]
    flow = [
        parts[1][0] - parts[-1][0],
        parts[0][1] + parts[1][1] + parts[-1][1],
        parts[0][2] + parts[1][2] + parts[-1][2],
    ]
    h = [value((ADJOINT, q)) for q in range(Q)]
    design, kinds = value((DESIGN, 0)), value((KIND, 0))
    return prepare(density, flow, design, kinds), h, design, kinds


def at(q, t):
    return pl.ds((q * (SIDES + 1) + t) * ROWS, ROWS)


def inner_kernel(wide, pop, por, kind, states, sense, ready):
    for t in range(SIDES):

        def value(entry, t=t):
            own = wide[pl.ds((X_AT[entry] * (EXT + 2) + t) * ROWS, ROWS), :]
            s = shift_of(entry)
            return pltpu.roll(own, s % NX, 1) if s else own

        back, by_porosity = pull_back(*later_adjoint(value), wanted_at(t))
        for q in wanted_at(t):
            states[at(q, t), :] = back[q]
        if 1 <= t <= NZ:
            sense[t - 1] = by_porosity
    for z in range(NZ):
        density, flow = moments([pop[q, z] for q in range(Q)])
        for i, part in enumerate(prepare(density, flow, por[z], kind[z])):
            ready[i, z] = part


def adjoint_kernel(states, sense, ready, packed, one, two, por, kind, out, sense_out, sides):
    lane = lax.broadcasted_iota(jnp.int32, (NY, NX), 1)
    row = lax.broadcasted_iota(jnp.int32, (NY, NX), 0)
    before, after = from_side("gx", one, two)
    slot = lane & 3
    ends = []
    for u in range(PACKED):
        s = shift_of(X_FIELDS[u * PER_TILE])
        own = packed[u]
        if s > 0:
            ends.append(jnp.where(slot < 2, own, pltpu.roll(before(u), 2, 1)))
        elif s < 0:
            ends.append(jnp.where(slot < 2, pltpu.roll(after(u), NX - 2, 1), own))
        else:
            here = jnp.where(slot == 1, own, after(u))
            there = jnp.where(slot == 1, before(u), own)
            ends.append(
                jnp.where(slot < 2, pltpu.roll(here, NX - 1, 1), pltpu.roll(there, 1, 1))
            )

    def value(entry):
        u, j = divmod(X_AT[entry], PER_TILE)
        return pltpu.roll(ends[u], NX - 32 * j, 1) if j else ends[u]

    def together(tile):
        return jnp.where(slot == 0, tile, pltpu.roll(tile, NX - 2, 1))

    back, by_porosity = pull_back(*later_adjoint(value), wanted_at(SIDES))
    for q in range(Q):
        sides[q] = back[q] if VELOCITIES[q][0] else together(back[q])
    by_porosity = together(by_porosity)
    last, first_two, last_two = lane == NX - 1, lane < 2, lane >= NX - 2
    outer = (lane == 0) | last

    def moved_x(q, t):
        tile = states[at(q, t), :]
        cx = VELOCITIES[q][0]
        if cx > 0:
            turned = pltpu.roll(sides[q], NX - 2 - 4 * t, 1)
            return jnp.where(last_two, turned, pltpu.roll(tile, NX - 1, 1))
        if cx < 0:
            turned = pltpu.roll(sides[q], NX - 2 - 4 * t, 1)
            return jnp.where(first_two, turned, pltpu.roll(tile, 1, 1))
        return jnp.where(outer, pltpu.roll(sides[q], NX - 1 - 4 * t, 1), tile)

    for z in range(NZ):
        h = []
        for q in range(Q):
            _, cy, cz = VELOCITIES[q]
            t = z + cz + 1
            tile = moved_x(q, t)
            if cy:
                edge = moved_x(q, HIGH if cy > 0 else LOW)[t : t + 1]
                tile = jnp.where(
                    row == (NY - 1 if cy > 0 else 0),
                    jnp.broadcast_to(edge, (NY, NX)),
                    pltpu.roll(tile, NY - 1 if cy > 0 else 1, 0),
                )
            h.append(tile)
        back, now = pull_back(
            [ready[i, z] for i in range(STATE)], h, por[z], kind[z], range(Q)
        )
        for q in range(Q):
            out[q, z] = back[q]
        then = jnp.where(outer, pltpu.roll(by_porosity, NX - 1 - 4 * (z + 1), 1), sense[z])
        sense_out[z] = then + now


VMEM = pl.BlockSpec(memory_space=pltpu.VMEM)
SMEM = pl.BlockSpec(memory_space=pltpu.SMEM)
HBM = pl.BlockSpec(memory_space=pltpu.HBM)


def call(kernel, shapes, specs, scratch=(), out_specs=None, cost=None):
    out = [
        shape if isinstance(shape, jax.ShapeDtypeStruct) else jax.ShapeDtypeStruct(shape, jnp.float32)
        for shape in shapes
    ]
    return pl.pallas_call(
        kernel,
        out_shape=out,
        in_specs=specs,
        out_specs=out_specs or [VMEM] * len(out),
        scratch_shapes=list(scratch),
        cost_estimate=cost,
        compiler_params=pltpu.CompilerParams(vmem_limit_bytes=12 * 1024 * 1024),
    )


def both_ways(first, second, axis):
    count = lax.axis_size(axis)
    if axis in SWAPPED:
        one = [(i, i ^ 1) for i in range(count)]
        two = [((i + 1) % count, ((i ^ 1) + 1) % count) for i in range(count)]
    else:
        one = [(i, i + 1) for i in range(count - 1)]
        two = [(t, s) for s, t in one]
    if axis != "gx":
        two = [(s, t) for s, t in two if abs(s - t) == 1]
    if axis in REVERSED:
        one, two = two, one
    return lax.ppermute(first, axis, one), lax.ppermute(second, axis, two)


def on_device(populations, porosity, node_type, step_index, adjoint_end):
    tile = (NY, NX)
    moved, first, second, pop, adj, por, kind = call(
        collide_kernel,
        [(Q, NZ, *tile), (len(Z_UP), *tile), (len(Z_DOWN), *tile)]
        + [(Q, NZ, *tile), (Q, NZ, *tile), (NZ, *tile), (NZ, *tile)],
        [SMEM] + [HBM] * 4,
        [pltpu.VMEM((NZ, *tile), jnp.int32), pltpu.SemaphoreType.DMA((4,))],
    )(
        step_index,
        *(
            pltpu.with_memory_space_constraint(x, pltpu.HBM)
            for x in (populations, adjoint_end, porosity, node_type)
        ),
    )
    one, two = both_ways(first, second, "gz")
    shifted, up, down, *copies = call(
        rows_kernel if "gy" in SWAPPED else functools.partial(without_copies, rows_kernel),
        [(len(Y_FIELDS) * EXT * ROWS, NX), (Y_UP_ROWS, NX), (Y_DOWN_ROWS, NX)]
        + [(Y_UP_ROWS, NX), (Y_DOWN_ROWS, NX)] * ("gy" in SWAPPED),
        [VMEM] * 6,
    )(moved, adj, por, kind, one, two)
    first, second = copies or (up, down)
    if "gy" in REVERSED and not copies:
        first, second = down, up
    one, two = both_ways(first, second, "gy")
    wide, packed = call(
        columns_kernel,
        [(len(X_FIELDS) * (EXT + 2) * ROWS, NX), (PACKED, *tile)],
        [VMEM] * 5,
    )(shifted, up, down, one, two)
    one, two = both_ways(packed, packed, "gx")
    states, part, ready = call(
        inner_kernel,
        [(Q * (SIDES + 1) * ROWS, NX), (NZ, *tile), (STATE, NZ, *tile)],
        [VMEM] * 4,
        cost=pl.CostEstimate(flops=20_000_000, bytes_accessed=4_000_000, transcendentals=0),
    )(wide, pop, por, kind)
    adjoint, sense = call(
        adjoint_kernel,
        [(Q, NZ, *tile), (NZ, *tile)],
        [VMEM] * 8,
        [pltpu.VMEM((Q, *tile), jnp.float32)],
    )(states, part, ready, packed, one, two, por, kind)
    return adjoint, sense


def without_copies(kernel, *refs):
    kernel(*refs, None, None)


def solution(mesh):
    brick = P(None, "gz", "gy", "gx")
    field = P("gz", "gy", "gx")
    return jax.shard_map(
        on_device,
        mesh=mesh,
        in_specs=(brick, field, field, P(), brick),
        out_specs=(brick, field),
        check_vma=False,
    )
```

```python
import functools
import math

import jax
import jax.numpy as jnp
from jax import lax
from jax.experimental import pallas as pl
from jax.experimental.pallas import tpu as pltpu
from jax.sharding import PartitionSpec as P

VELOCITIES = (
    (0, 0, 0),
    (1, 0, 0),
    (-1, 0, 0),
    (0, 1, 0),
    (0, -1, 0),
    (0, 0, 1),
    (0, 0, -1),
    (1, 1, 0),
    (-1, -1, 0),
    (1, -1, 0),
    (-1, 1, 0),
    (1, 0, 1),
    (-1, 0, -1),
    (1, 0, -1),
    (-1, 0, 1),
    (0, 1, 1),
    (0, -1, -1),
    (0, 1, -1),
    (0, -1, 1),
)
WEIGHTS = (1.0 / 3.0,) + (1.0 / 18.0,) * 6 + (1.0 / 36.0,) * 12
OPPOSITE = (0, 2, 1, 4, 3, 6, 5, 8, 7, 10, 9, 12, 11, 14, 13, 16, 15, 18, 17)
Q = 19
RATE = 1.25
RAMP = 0.1
NZ, NY, NX = 4, 8, 128
EXT = NZ + 2
LOW, HIGH = EXT, EXT + 1
SIDES = EXT + 2
ROWS = 8
SWAPPED = ("gx",)
REVERSED = ("gz",)

FLUID, WALL, INLET, OUTLET = -1, 0, 1, 2

FORWARD, ADJOINT, DESIGN, KIND = range(4)


def opposed(c):
    return tuple(-i for i in c)


Z_FIELDS = (
    [(FORWARD, q, VELOCITIES[q][2]) for q in range(Q)]
    + [(ADJOINT, q, -VELOCITIES[q][2]) for q in range(Q)]
    + [(DESIGN, 0, 0), (KIND, 0, 0)]
)
Z_UP, Z_DOWN = [], []
for _what, _which, _s in Z_FIELDS:
    if _s >= 0:
        Z_UP += [(_what, _which, p) for p in range(NZ - 1 - _s, NZ)]
    if _s <= 0:
        Z_DOWN += [(_what, _which, p) for p in range(0, 1 - _s)]
Z_UP_AT = {entry: i for i, entry in enumerate(Z_UP)}
Z_DOWN_AT = {entry: i for i, entry in enumerate(Z_DOWN)}

Y_FIELDS = []
for _cy in (-1, 0, 1):
    for _cx in (-1, 0, 1):
        _same = [q for q in range(Q) if VELOCITIES[q][:2] == (_cx, _cy)]
        Y_FIELDS.append((FORWARD, (_cx, _cy, 0), [(1, q) for q in _same], _cy))
        _deep = [(VELOCITIES[q][2], q) for q in _same if VELOCITIES[q][2]]
        if _deep:
            Y_FIELDS.append((FORWARD, (_cx, _cy, 1), _deep, _cy))
Y_FIELDS += [(ADJOINT, q, [(1, q)], -VELOCITIES[q][1]) for q in range(Q)]
Y_FIELDS += [(DESIGN, 0, [(1, 0)], 0), (KIND, 0, [(1, 0)], 0)]
Y_AT = {(what, which): i for i, (what, which, _, _) in enumerate(Y_FIELDS)}
Y_UP, Y_DOWN = [], []
for _i, (_, _, _, _s) in enumerate(Y_FIELDS):
    if _s >= 0:
        Y_UP += [(_i, row) for row in range(NY - 1 - _s, NY)]
    if _s <= 0:
        Y_DOWN += [(_i, row) for row in range(0, 1 - _s)]
Y_UP_AT = {entry: i for i, entry in enumerate(Y_UP)}
Y_DOWN_AT = {entry: i for i, entry in enumerate(Y_DOWN)}


def padded(rows):
    return -(-(rows + 2) // ROWS) * ROWS


Y_UP_ROWS, Y_DOWN_ROWS = padded(len(Y_UP) * EXT), padded(len(Y_DOWN) * EXT)

X_FIELDS = []
for _s in (1, -1, 0):
    X_FIELDS += [(FORWARD, (_s, i)) for i in range(3)]
    X_FIELDS += [(ADJOINT, q) for q in range(Q) if -VELOCITIES[q][0] == _s]
X_FIELDS += [(DESIGN, 0), (KIND, 0)]
X_AT = {entry: i for i, entry in enumerate(X_FIELDS)}
PER_TILE = 4
PACKED = -(-len(X_FIELDS) // PER_TILE)


def shift_of(entry):
    what, which = entry
    if what == FORWARD:
        return which[0]
    return -VELOCITIES[which][0] if what == ADJOINT else 0


def add_up(terms):
    total = None
    for sign, value in terms:
        if total is None:
            total = value if sign > 0 else -value
        else:
            total = total + value if sign > 0 else total - value
    return total


def moments(f):
    density = add_up([(1, f[q]) for q in range(Q)])
    flow = [
        add_up([(VELOCITIES[q][i], f[q]) for q in range(Q) if VELOCITIES[q][i]])
        for i in range(3)
    ]
    return density, flow


def along(q, vector):
    return add_up([(VELOCITIES[q][i], vector[i]) for i in range(3) if VELOCITIES[q][i]])


def collide(f, porosity, kinds, speed):
    density, flow = moments(f)
    inverse = 1.0 / density
    fluid = kinds == FLUID
    wall = kinds == WALL
    inlet = kinds == INLET
    damping = RAMP * (1.0 - porosity) / (RAMP + porosity)
    kept = jnp.where(fluid, 1.0 - damping, 1.0)
    v = [
        jnp.where(inlet, speed if i == 0 else 0.0, flow[i] * inverse * kept)
        for i in range(3)
    ]
    r = jnp.where(inlet, 1.0, density)
    scale = jnp.where(fluid, RATE, 1.0) * r
    keep = jnp.where(fluid, 1.0 - RATE, 0.0)
    base = 1.0 - 1.5 * (v[0] * v[0] + v[1] * v[1] + v[2] * v[2])
    out = []
    for q in range(Q):
        p = along(q, v)
        shape = base if p is None else base + p * (3.0 + 4.5 * p)
        moved = keep * f[q] + (WEIGHTS[q] * scale) * shape
        out.append(jnp.where(wall, f[OPPOSITE[q]], moved))
    return out


def prepare(density, flow, porosity, kinds):
    inverse = 1.0 / density
    return [density, *(flow[i] * inverse for i in range(3)), 1.0 / (RAMP + porosity)]


def pull_back(state, h, porosity, kinds, wanted):
    density, *u, ramp = state
    fluid = kinds == FLUID
    wall = kinds == WALL
    outlet = kinds == OUTLET
    square = u[0] * u[0] + u[1] * u[1] + u[2] * u[2]
    damping = jnp.where(fluid, RAMP * (1.0 - porosity) * ramp, 0.0)
    kept = 1.0 - damping
    v = [kept * u[i] for i in range(3)]
    face, edge = WEIGHTS[1], WEIGHTS[7]
    plus = {}
    minus = {}
    for q in range(1, Q, 2):
        plus[q] = h[q] + h[q + 1]
        minus[q] = h[q] - h[q + 1]
    xy, yx, xz, zx, yz, zy = (plus[q] for q in (7, 9, 11, 13, 15, 17))
    second = [
        [face * plus[1] + edge * ((xy + yx) + (xz + zx)), edge * (xy - yx), edge * (xz - zx)],
        [None, face * plus[3] + edge * ((xy + yx) + (yz + zy)), edge * (yz - zy)],
        [None, None, face * plus[5] + edge * ((xz + zx) + (yz + zy))],
    ]
    second[1][0], second[2][0], second[2][1] = second[0][1], second[0][2], second[1][2]
    zero = (
        WEIGHTS[0] * h[0]
        + face * (plus[1] + plus[3] + plus[5])
        + edge * ((xy + yx) + (xz + zx) + (yz + zy))
    )
    first = [
        face * minus[1] + edge * ((minus[7] + minus[9]) + (minus[11] + minus[13])),
        face * minus[3] + edge * ((minus[7] - minus[9]) + (minus[15] + minus[17])),
        face * minus[5] + edge * ((minus[11] - minus[13]) + (minus[15] - minus[17])),
    ]
    bent = [
        4.5 * (second[i][0] * v[0] + second[i][1] * v[1] + second[i][2] * v[2])
        - 1.5 * zero * v[i]
        for i in range(3)
    ]
    level = zero + sum(v[i] * (3.0 * first[i] + bent[i]) for i in range(3))
    slope = [3.0 * first[i] + 2.0 * bent[i] for i in range(3)]
    rate = jnp.where(fluid, RATE, jnp.where(outlet, 1.0, 0.0))
    keep = jnp.where(fluid, 1.0 - RATE, 0.0)
    turn = sum(slope[i] * u[i] for i in range(3))
    moved_rate = rate * kept
    tilt = [moved_rate * slope[i] + 2.0 * damping * u[i] for i in range(3)]
    flat = rate * level - moved_rate * turn - damping * square
    out = {}
    for q in wanted:
        p = along(q, tilt)
        moved = keep * h[q] + (flat if p is None else flat + p)
        out[q] = jnp.where(wall, h[OPPOSITE[q]], moved)
    by_porosity = jnp.where(
        fluid,
        (-RAMP * (1.0 + RAMP)) * ramp * ramp * density * (square - RATE * turn),
        0.0,
    )
    return out, by_porosity


def by_side(axis, act, first, second):
    if axis in REVERSED:
        first, second = second, first
    if axis not in SWAPPED:
        act(first, second)
        return
    here = lax.rem(lax.axis_index(axis), 2)

    @pl.when(here == 0)
    def _():
        act(first, second)

    @pl.when(here == 1)
    def _():
        act(second, first)


def from_side(axis, first, second):
    if axis in REVERSED:
        first, second = second, first
    if axis not in SWAPPED:
        return (lambda at: first[at]), (lambda at: second[at])
    even = lax.rem(lax.axis_index(axis), 2) == 0
    return (
        lambda at: jnp.where(even, second[at], first[at]),
        lambda at: jnp.where(even, first[at], second[at]),
    )


def collide_kernel(
    step, pop_hbm, adj_hbm, por_hbm, kind_hbm, moved, first, second, pop, adj, por, kind, raw, done
):
    copies = [
        pltpu.make_async_copy(source, target, done.at[i])
        for i, (source, target) in enumerate(
            ((pop_hbm, pop), (por_hbm, por), (kind_hbm, raw), (adj_hbm, adj))
        )
    ]
    for copy in copies:
        copy.start()
    moment = jnp.full((NY, NX), step[0] & 63, jnp.int32).astype(jnp.float32)
    speed = 0.1 * (1.0 + 0.8 * jnp.sin((2.0 * math.pi / 64.0) * moment))
    for copy in copies[:3]:
        copy.wait()
    for z in range(NZ):
        kind[z] = (raw[z] - 1).astype(jnp.float32)
        collided = collide([pop[q, z] for q in range(Q)], por[z], kind[z], speed)
        for q in range(Q):
            moved[q, z] = collided[q]
    copies[3].wait()

    def value(what, which, z):
        if what == FORWARD:
            return moved[which, z]
        if what == ADJOINT:
            return adj[which, z]
        return por[z] if what == DESIGN else kind[z]

    def write(up, down):
        for table, out in ((Z_UP_AT, up), (Z_DOWN_AT, down)):
            for entry, at in table.items():
                out[at] = value(*entry)

    by_side("gz", write, first, second)


def copy_both(up, down, first, second):
    for i in range(up.shape[0] // ROWS):
        rows = pl.ds(i * ROWS, ROWS)
        first[rows, :] = up[rows, :]
        second[rows, :] = down[rows, :]


def rows_kernel(moved, adj, por, kind, one, two, shifted, up, down, first, second):
    below, above = from_side("gz", one, two)

    def plane_of(what, which, z):
        if z < 0:
            return below(Z_UP_AT[what, which, z + NZ])
        if z >= NZ:
            return above(Z_DOWN_AT[what, which, z - NZ])
        if what == FORWARD:
            return moved[which, z]
        if what == ADJOINT:
            return adj[which, z]
        return por[z] if what == DESIGN else kind[z]

    for i, (what, _, parts, _) in enumerate(Y_FIELDS):
        for t in range(EXT):
            terms = []
            for sign, q in parts:
                s = VELOCITIES[q][2] if what == FORWARD else 0
                if what == ADJOINT:
                    s = -VELOCITIES[q][2]
                terms.append((sign, plane_of(what, q, t - 1 - s)))
            shifted[pl.ds((i * EXT + t) * ROWS, ROWS), :] = add_up(terms)
    def write(forward, backward):
        for table, out in ((Y_UP, forward), (Y_DOWN, backward)):
            for at, (i, row) in enumerate(table):
                out[pl.ds(at * EXT, EXT), :] = shifted[
                    pl.ds(i * EXT * ROWS + row, EXT, stride=ROWS), :
                ]
            used = len(table) * EXT
            out[pl.ds(used, out.shape[0] - used), :] = jnp.zeros(
                (out.shape[0] - used, NX), jnp.float32
            )

    write(up, down)
    if "gy" in SWAPPED:
        by_side("gy", functools.partial(copy_both, up, down), first, second)


def columns_kernel(shifted, up, down, one, two, wide, packed, first, second):
    left, right = from_side("gy", one, two)
    row = lax.broadcasted_iota(jnp.int32, (NY, NX), 0)
    lane = lax.broadcasted_iota(jnp.int32, (NY, NX), 1)

    def rows_of(ref, at):
        rows = (pl.ds(at * EXT, ROWS), slice(None))
        return ref(rows) if callable(ref) else ref[rows]

    def row_of(ref, at, t):
        return jnp.broadcast_to(ref((pl.ds(at * EXT + t, 1), slice(None))), (NY, NX))

    def tile_of(entry, t):
        i = Y_AT[entry]
        s = Y_FIELDS[i][3]
        if t == LOW:
            if s < 0:
                return rows_of(down, Y_DOWN_AT[i, 0])
            return rows_of(left, Y_UP_AT[i, NY - 1 - s])
        if t == HIGH:
            if s > 0:
                return rows_of(up, Y_UP_AT[i, NY - 1])
            return rows_of(right, Y_DOWN_AT[i, -s])
        own = shifted[pl.ds((i * EXT + t) * ROWS, ROWS), :]
        if s > 0:
            return jnp.where(
                row == 0, row_of(left, Y_UP_AT[i, NY - 1], t), pltpu.roll(own, 1, 0)
            )
        if s < 0:
            return jnp.where(
                row == NY - 1, row_of(right, Y_DOWN_AT[i, 0], t), pltpu.roll(own, NY - 1, 0)
            )
        return own

    for u in range(PACKED):
        total = None
        for j, entry in enumerate(X_FIELDS[u * PER_TILE : (u + 1) * PER_TILE]):
            f = u * PER_TILE + j
            what, which = entry
            for t in range(EXT + 2):
                if what != FORWARD:
                    tile = tile_of(entry, t)
                else:
                    cx, part = which
                    terms = []
                    for cy in (-1, 0, 1):
                        source = (FORWARD, (cx, cy, 1 if part == 2 else 0))
                        if source in Y_AT and (part != 1 or cy):
                            sign = cy if part == 1 else 1
                            terms.append((sign, tile_of(source, t)))
                    tile = add_up(terms)
                wide[pl.ds((f * (EXT + 2) + t) * ROWS, ROWS), :] = tile
                k = j * (EXT + 2) + t
                turned = pltpu.roll(tile, (2 + 4 * k) % NX, 1)
                total = turned if total is None else jnp.where(lane >= 4 * k, turned, total)
        packed[u] = total

    def write(forward, backward):
        low = (lane & 3) < 2
        for v in range(PACKED // 2):
            one_, two_ = packed[2 * v], packed[2 * v + 1]
            forward[v] = jnp.where(low, one_, pltpu.roll(two_, 2, 1))
            backward[v] = jnp.where(low, pltpu.roll(one_, NX - 2, 1), two_)

    by_side("gx", write, first, second)


STATE = 5


def wanted_at(t):
    if t == SIDES:
        return list(range(Q))
    if t in (LOW, HIGH):
        return [q for q in range(Q) if VELOCITIES[q][1] == (1 if t == HIGH else -1)]
    if t in (0, EXT - 1):
        return [q for q in range(Q) if VELOCITIES[q][2] == (1 if t else -1)]
    return list(range(Q))


def later_adjoint(value):
    parts = {s: [value((FORWARD, (s, i))) for i in range(3)] for s in (-1, 0, 1)}
    density = parts[0][0] + parts[1][0] + parts[-1][0]
    flow = [
        parts[1][0] - parts[-1][0],
        parts[0][1] + parts[1][1] + parts[-1][1],
        parts[0][2] + parts[1][2] + parts[-1][2],
    ]
    h = [value((ADJOINT, q)) for q in range(Q)]
    design, kinds = value((DESIGN, 0)), value((KIND, 0))
    return prepare(density, flow, design, kinds), h, design, kinds


def at(q, t):
    return pl.ds((q * (SIDES + 1) + t) * ROWS, ROWS)


def inner_kernel(wide, pop, por, kind, states, sense, ready):
    for t in range(SIDES):

        def value(entry, t=t):
            own = wide[pl.ds((X_AT[entry] * (EXT + 2) + t) * ROWS, ROWS), :]
            s = shift_of(entry)
            return pltpu.roll(own, s % NX, 1) if s else own

        back, by_porosity = pull_back(*later_adjoint(value), wanted_at(t))
        for q in wanted_at(t):
            states[at(q, t), :] = back[q]
        if 1 <= t <= NZ:
            sense[t - 1] = by_porosity
    for z in range(NZ):
        density, flow = moments([pop[q, z] for q in range(Q)])
        for i, part in enumerate(prepare(density, flow, por[z], kind[z])):
            ready[i, z] = part


def adjoint_kernel(states, sense, ready, packed, one, two, por, kind, out, sense_out, sides):
    lane = lax.broadcasted_iota(jnp.int32, (NY, NX), 1)
    row = lax.broadcasted_iota(jnp.int32, (NY, NX), 0)
    low_half, high_half = from_side("gx", one, two)

    def before(u):
        return pltpu.roll(low_half(u // 2), NX - 2, 1) if u % 2 else low_half(u // 2)

    def after(u):
        return high_half(u // 2) if u % 2 else pltpu.roll(high_half(u // 2), 2, 1)

    slot = lane & 3
    ends = []
    for u in range(PACKED):
        s = shift_of(X_FIELDS[u * PER_TILE])
        own = packed[u]
        if s > 0:
            ends.append(jnp.where(slot < 2, own, pltpu.roll(before(u), 2, 1)))
        elif s < 0:
            ends.append(jnp.where(slot < 2, pltpu.roll(after(u), NX - 2, 1), own))
        else:
            here = jnp.where(slot == 1, own, after(u))
            there = jnp.where(slot == 1, before(u), own)
            ends.append(
                jnp.where(slot < 2, pltpu.roll(here, NX - 1, 1), pltpu.roll(there, 1, 1))
            )

    def value(entry):
        u, j = divmod(X_AT[entry], PER_TILE)
        return pltpu.roll(ends[u], NX - 32 * j, 1) if j else ends[u]

    def together(tile):
        return jnp.where(slot == 0, tile, pltpu.roll(tile, NX - 2, 1))

    back, by_porosity = pull_back(*later_adjoint(value), wanted_at(SIDES))
    for q in range(Q):
        sides[q] = back[q] if VELOCITIES[q][0] else together(back[q])
    by_porosity = together(by_porosity)
    last, first_two, last_two = lane == NX - 1, lane < 2, lane >= NX - 2
    outer = (lane == 0) | last

    def moved_x(q, t):
        tile = states[at(q, t), :]
        cx = VELOCITIES[q][0]
        if cx > 0:
            turned = pltpu.roll(sides[q], NX - 2 - 4 * t, 1)
            return jnp.where(last_two, turned, pltpu.roll(tile, NX - 1, 1))
        if cx < 0:
            turned = pltpu.roll(sides[q], NX - 2 - 4 * t, 1)
            return jnp.where(first_two, turned, pltpu.roll(tile, 1, 1))
        return jnp.where(outer, pltpu.roll(sides[q], NX - 1 - 4 * t, 1), tile)

    for z in range(NZ):
        h = []
        for q in range(Q):
            _, cy, cz = VELOCITIES[q]
            t = z + cz + 1
            tile = moved_x(q, t)
            if cy:
                edge = moved_x(q, HIGH if cy > 0 else LOW)[t : t + 1]
                tile = jnp.where(
                    row == (NY - 1 if cy > 0 else 0),
                    jnp.broadcast_to(edge, (NY, NX)),
                    pltpu.roll(tile, NY - 1 if cy > 0 else 1, 0),
                )
            h.append(tile)
        back, now = pull_back(
            [ready[i, z] for i in range(STATE)], h, por[z], kind[z], range(Q)
        )
        for q in range(Q):
            out[q, z] = back[q]
        then = jnp.where(outer, pltpu.roll(by_porosity, NX - 1 - 4 * (z + 1), 1), sense[z])
        sense_out[z] = then + now


VMEM = pl.BlockSpec(memory_space=pltpu.VMEM)
SMEM = pl.BlockSpec(memory_space=pltpu.SMEM)
HBM = pl.BlockSpec(memory_space=pltpu.HBM)


def call(kernel, shapes, specs, scratch=(), out_specs=None, cost=None):
    out = [
        shape if isinstance(shape, jax.ShapeDtypeStruct) else jax.ShapeDtypeStruct(shape, jnp.float32)
        for shape in shapes
    ]
    return pl.pallas_call(
        kernel,
        out_shape=out,
        in_specs=specs,
        out_specs=out_specs or [VMEM] * len(out),
        scratch_shapes=list(scratch),
        cost_estimate=cost,
        compiler_params=pltpu.CompilerParams(vmem_limit_bytes=12 * 1024 * 1024),
    )


def both_ways(first, second, axis):
    count = lax.axis_size(axis)
    if axis in SWAPPED:
        one = [(i, i ^ 1) for i in range(count)]
        two = [((i + 1) % count, ((i ^ 1) + 1) % count) for i in range(count)]
    else:
        one = [(i, i + 1) for i in range(count - 1)]
        two = [(t, s) for s, t in one]
    if axis != "gx":
        two = [(s, t) for s, t in two if abs(s - t) == 1]
    if axis in REVERSED:
        one, two = two, one
    return lax.ppermute(first, axis, one), lax.ppermute(second, axis, two)


def on_device(populations, porosity, node_type, step_index, adjoint_end):
    tile = (NY, NX)
    moved, first, second, pop, adj, por, kind = call(
        collide_kernel,
        [(Q, NZ, *tile), (len(Z_UP), *tile), (len(Z_DOWN), *tile)]
        + [(Q, NZ, *tile), (Q, NZ, *tile), (NZ, *tile), (NZ, *tile)],
        [SMEM] + [HBM] * 4,
        [pltpu.VMEM((NZ, *tile), jnp.int32), pltpu.SemaphoreType.DMA((4,))],
    )(
        step_index,
        *(
            pltpu.with_memory_space_constraint(x, pltpu.HBM)
            for x in (populations, adjoint_end, porosity, node_type)
        ),
    )
    one, two = both_ways(first, second, "gz")
    shifted, up, down, *copies = call(
        rows_kernel if "gy" in SWAPPED else functools.partial(without_copies, rows_kernel),
        [(len(Y_FIELDS) * EXT * ROWS, NX), (Y_UP_ROWS, NX), (Y_DOWN_ROWS, NX)]
        + [(Y_UP_ROWS, NX), (Y_DOWN_ROWS, NX)] * ("gy" in SWAPPED),
        [VMEM] * 6,
    )(moved, adj, por, kind, one, two)
    first, second = copies or (up, down)
    if "gy" in REVERSED and not copies:
        first, second = down, up
    one, two = both_ways(first, second, "gy")
    wide, packed, first, second = call(
        columns_kernel,
        [(len(X_FIELDS) * (EXT + 2) * ROWS, NX), (PACKED, *tile)] + [(PACKED // 2, *tile)] * 2,
        [VMEM] * 5,
    )(shifted, up, down, one, two)
    one, two = both_ways(first, second, "gx")
    states, part, ready = call(
        inner_kernel,
        [(Q * (SIDES + 1) * ROWS, NX), (NZ, *tile), (STATE, NZ, *tile)],
        [VMEM] * 4,
        cost=pl.CostEstimate(flops=20_000_000, bytes_accessed=4_000_000, transcendentals=0),
    )(wide, pop, por, kind)
    adjoint, sense = call(
        adjoint_kernel,
        [(Q, NZ, *tile), (NZ, *tile)],
        [VMEM] * 8,
        [pltpu.VMEM((Q, *tile), jnp.float32)],
    )(states, part, ready, packed, one, two, por, kind)
    return adjoint, sense


def without_copies(kernel, *refs):
    kernel(*refs, None, None)


def solution(mesh):
    brick = P(None, "gz", "gy", "gx")
    field = P("gz", "gy", "gx")
    return jax.shard_map(
        on_device,
        mesh=mesh,
        in_specs=(brick, field, field, P(), brick),
        out_specs=(brick, field),
        check_vma=False,
    )
```
